768 devices in a mesh: sec: 192 (over y, z, core), band: 4 (over x).
Axes of the slice: x: 4, y: 8, z: 12, core: 2. Of those that a mesh axis runs over, the one named last changes fastest.
Arguments:
- targets: bfloat16 [2, 160, 192, 4, 512], P(None, None, 'sec', 'band'), may hold values from -36 to 36
- coords: bfloat16 [4, 160, 192, 4, 512], P(None, None, 'sec', 'band'), may hold values from -1 to 1
- pair_first: int32 [192, 4, 512], P('sec', 'band'), may hold values from 1792 to 2815, as said below
- pair_second: int32 [192, 4, 512], P('sec', 'band'), may hold values from 0 to 4607, as said below
- pair_count: int32 [192, 4, 512], P('sec', 'band'), may hold values from 37 to 150, as said below
Outputs:
- solution: float32 [6, 384, 8, 128], P(None, 'sec', 'band')
- next_direction: float32 [6, 384, 8, 128], P(None, 'sec', 'band')
The draws below stay inside these ranges and needn't reach their ends.
Inputs may be any that keep to these rules, and one draw needn't show every extreme that they name: `pair_first`: for each slab and band the 512 entries name every tile of that slab's and band's own block once, as ((s + 2) * 6 + r + 2) * 128 + c for local section s, row r and column c. `pair_second`: an index of the same form naming a tile of the grid other than the pair's first, at most two sections, two rows and two columns away from it; every other pair lies within one section. `pair_count`: each slab and band has a pair with exactly 150 matches.
All inputs are finite; a program needn't handle non-finite values.
Results may differ from the reference program's by a relative error of at most 0.0012.
Values sent between devices are 32-bit elements; how exact they have to be, the bound alone decides.
A program may use at most 32 MiB of HBM per device.

```python
import math
import jax
import jax.numpy as jnp
from jax import lax

NCOLS = 128
SEC_DEV = 2
ROWS_DEV = 2
MATCH_CAP = 160
MATCHES = 150
NSLAB = 192
NBAND = 4
NSEC = 384
NROWS = 8
PAIRS_DEV = 512


def pair_tables(key):
    tile_count = SEC_DEV * ROWS_DEV * NCOLS
    rows_wide = ROWS_DEV + 4
    grid_shape = (NSLAB, NBAND, tile_count)
    key_order, key_row, key_col, key_sec, key_sign = jax.random.split(key, 5)
    position = lax.broadcasted_iota(jnp.int32, grid_shape, 2)
    scores = jax.random.randint(key_order, grid_shape, 0, 1024) * tile_count + position
    local_tile = jnp.argsort(scores, axis=-1).astype(jnp.int32)
    section = local_tile // (ROWS_DEV * NCOLS)
    row_local = local_tile // NCOLS % ROWS_DEV
    column = local_tile % NCOLS
    slab_ids = lax.broadcasted_iota(jnp.int32, grid_shape, 0)
    band_ids = lax.broadcasted_iota(jnp.int32, grid_shape, 1)
    cross_pair = position % 2 == 1
    step_row = jax.random.randint(key_row, grid_shape, -2, 3)
    step_col = jax.random.randint(key_col, grid_shape, -2, 3)
    step_sec = jax.random.randint(key_sec, grid_shape, 1, 3) * (2 * jax.random.randint(key_sign, grid_shape, 0, 2) - 1)
    step_sec = jnp.where(cross_pair, step_sec, 0)
    step_col = jnp.where(jnp.logical_and(jnp.logical_not(cross_pair), jnp.logical_and(step_row == 0, step_col == 0)), 1, step_col)
    section_global = slab_ids * SEC_DEV + section
    row_global = band_ids * ROWS_DEV + row_local
    step_sec = jnp.where(jnp.logical_or(section_global + step_sec < 0, section_global + step_sec >= NSEC), -step_sec, step_sec)
    step_row = jnp.where(jnp.logical_or(row_global + step_row < 0, row_global + step_row >= NROWS), -step_row, step_row)
    step_col = jnp.where(jnp.logical_or(column + step_col < 0, column + step_col >= NCOLS), -step_col, step_col)
    first_index = ((section + 2) * rows_wide + row_local + 2) * NCOLS + column
    second_index = ((section + step_sec + 2) * rows_wide + row_local + step_row + 2) * NCOLS + column + step_col
    return (first_index.astype(jnp.int32), second_index.astype(jnp.int32))


def draw_pair_first(key, part):
    tables = pair_tables(key)
    return tables[0]


def draw_pair_second(key, part):
    tables = pair_tables(key)
    return tables[1]


def draw_pair_count(key, part):
    key = jax.random.fold_in(key, 3)
    counts = jax.random.randint(key, (NSLAB, NBAND, PAIRS_DEV), MATCHES // 4, MATCHES + 1)
    return counts.at[:, :, 0].set(MATCHES).astype(jnp.int32)


def draw_targets(key, part):
    key = jax.random.fold_in(key, 4)
    key_base, key_scale = jax.random.split(key)
    full_shape = (2, MATCH_CAP, NSLAB, NBAND, PAIRS_DEV)
    base = jnp.clip(jax.random.normal(key_base, full_shape, jnp.float32), -4.0, 4.0)
    pair_scale = jnp.power(10.0, jax.random.uniform(key_scale, (NSLAB, NBAND, PAIRS_DEV), jnp.float32))
    slab_rise = 1.0 + 2.0 * lax.broadcasted_iota(jnp.float32, (NSLAB, 1, 1), 0) / max(NSLAB - 1, 1)
    values = 0.3 * base * (pair_scale * slab_rise)[None, None]
    return values.astype(jnp.bfloat16)


def steps_of(key, extent, cuts, smallest, high):
    factor_of = 1.0
    for dim, shards_of in cuts:
        steps = jax.random.uniform(jax.random.fold_in(jax.random.fold_in(key, 6), dim), (shards_of,), jnp.float32, smallest / len(cuts), high / len(cuts))
        factor_of = factor_of * jnp.repeat(jnp.exp(steps), extent[dim] // shards_of).reshape((-1,) + (1,) * (len(extent) - 1 - dim))
    return factor_of


def setup_inputs(seed: int = 0) -> dict:
    seeds = jax.random.split(jax.random.key(seed), 6)
    return {
        "targets": draw_targets(jax.random.fold_in(seeds[5], 71), 0),
        "coords": jnp.clip(jax.random.uniform(seeds[1], (4, MATCH_CAP, NSLAB, NBAND, PAIRS_DEV), jnp.float32, -1.0, 1.0) * steps_of(seeds[1], (4, MATCH_CAP, NSLAB, NBAND, PAIRS_DEV), ((2, 192), (3, 4)), -0.4, 0.0), -1.0, 1.0).astype(jnp.bfloat16),
        "pair_first": draw_pair_first(jax.random.fold_in(seeds[5], 71), 0),
        "pair_second": draw_pair_second(jax.random.fold_in(seeds[5], 71), 0),
        "pair_count": draw_pair_count(jax.random.fold_in(seeds[5], 71), 0),
    }


def global_tile(local, slab_index, band_index):
    rows_wide = ROWS_DEV + 4
    section = local // (rows_wide * NCOLS)
    row_local = local // NCOLS % rows_wide
    column = local % NCOLS
    section_global = slab_index * SEC_DEV + section - 2
    row_global = band_index * ROWS_DEV + row_local - 2
    return ((section_global * NROWS + row_global) * NCOLS + column).astype(jnp.int32)

def errors(params, near_index, far_index, points, present):
    near_params = params[:, near_index]
    far_params = params[:, far_index]
    error_x = near_params[0] * points[0] + near_params[1] * points[1] + near_params[2] - (far_params[0] * points[2] + far_params[1] * points[3] + far_params[2])
    error_y = near_params[3] * points[0] + near_params[4] * points[1] + near_params[5] - (far_params[3] * points[2] + far_params[4] * points[3] + far_params[5])
    return (jnp.where(present, error_x, 0.0), jnp.where(present, error_y, 0.0))

def spread(gradient, error_x, error_y, points, near_index, far_index):
    near_terms = jnp.stack([lax.optimization_barrier(jnp.sum(error_x * points[0], axis=0)), lax.optimization_barrier(jnp.sum(error_x * points[1], axis=0)), lax.optimization_barrier(jnp.sum(error_x, axis=0)), lax.optimization_barrier(jnp.sum(error_y * points[0], axis=0)), lax.optimization_barrier(jnp.sum(error_y * points[1], axis=0)), lax.optimization_barrier(jnp.sum(error_y, axis=0))])
    far_terms = jnp.stack([lax.optimization_barrier(jnp.sum(error_x * points[2], axis=0)), lax.optimization_barrier(jnp.sum(error_x * points[3], axis=0)), lax.optimization_barrier(jnp.sum(error_x, axis=0)), lax.optimization_barrier(jnp.sum(error_y * points[2], axis=0)), lax.optimization_barrier(jnp.sum(error_y * points[3], axis=0)), lax.optimization_barrier(jnp.sum(error_y, axis=0))])
    return gradient.at[:, near_index].add(near_terms).at[:, far_index].add(-far_terms)

def reference(targets, coords, pair_first, pair_second, pair_count):
    slab_ids = lax.broadcasted_iota(jnp.int32, (NSLAB, NBAND, PAIRS_DEV), 0)
    band_ids = lax.broadcasted_iota(jnp.int32, (NSLAB, NBAND, PAIRS_DEV), 1)
    near_all = global_tile(pair_first, slab_ids, band_ids)
    far_all = global_tile(pair_second, slab_ids, band_ids)
    tile_total = NSEC * NROWS * NCOLS
    slot_rows = lax.broadcasted_iota(jnp.int32, (MATCH_CAP, NBAND, PAIRS_DEV), 0)

    def slab_inputs(slab_index):
        points = lax.dynamic_slice_in_dim(coords, slab_index, 1, 2)[:, :, 0].astype(jnp.float32)
        target = lax.dynamic_slice_in_dim(targets, slab_index, 1, 2)[:, :, 0].astype(jnp.float32)
        present = slot_rows < pair_count[slab_index][None]
        target = jnp.where(present[None], target, 0.0)
        return (points, target, present, near_all[slab_index], far_all[slab_index])

    def first_pass(state_pair, slab_index):
        squares, gradient = state_pair
        points, target, present, near_index, far_index = slab_inputs(slab_index)
        squares = squares + jnp.sum(target * target)
        gradient = spread(gradient, target[0], target[1], points, near_index, far_index)
        return ((squares, gradient), None)
    zero_grad = jnp.zeros((6, tile_total), jnp.float32)
    slab_list = jnp.arange(NSLAB).astype(jnp.int32)
    (squares, gradient), _ = lax.scan(first_pass, (jnp.zeros((), jnp.float32), zero_grad), slab_list)
    beta_one = jnp.sqrt(squares)
    t_one = gradient / beta_one
    alpha_one = jnp.sqrt(jnp.sum(t_one * t_one))
    v_one = t_one / alpha_one

    def second_pass(state_pair, slab_index):
        squares, gradient = state_pair
        points, target, present, near_index, far_index = slab_inputs(slab_index)
        image_x, image_y = errors(v_one, near_index, far_index, points, present)
        hat_x = image_x - alpha_one * (target[0] / beta_one)
        hat_y = image_y - alpha_one * (target[1] / beta_one)
        squares = squares + jnp.sum(hat_x * hat_x) + jnp.sum(hat_y * hat_y)
        gradient = spread(gradient, hat_x, hat_y, points, near_index, far_index)
        return ((squares, gradient), None)
    (squares, gradient), _ = lax.scan(second_pass, (jnp.zeros((), jnp.float32), zero_grad), slab_list)
    beta_two = jnp.sqrt(squares)
    t_two = gradient / beta_two - beta_two * v_one
    alpha_two = jnp.sqrt(jnp.sum(t_two * t_two))
    v_two = t_two / alpha_two
    rho_square = alpha_one * alpha_one + beta_two * beta_two
    solution = alpha_one * beta_one / rho_square * v_one
    direction = math.sqrt(6.0 * tile_total) * (v_two - beta_two * alpha_two / rho_square * v_one)
    grid_shape = (6, NSEC, NROWS, NCOLS)
    return (solution.reshape(grid_shape), direction.reshape(grid_shape))
```

```python
import functools
import math

import jax
import jax.numpy as jnp
from jax import lax
from jax.experimental import pallas as pl
from jax.experimental.pallas import tpu as pltpu
from jax.sharding import PartitionSpec as P

NCOLS = 128
SEC_DEV = 2
ROWS_DEV = 2
TILE_ROWS = SEC_DEV * ROWS_DEV
ROWS_WIDE = ROWS_DEV + 4
MESH = pl.DeviceIdType.MESH
F32 = jnp.float32
SHIFTS = (-2, -1, 0, 1, 2)
NEIGHBOURS = tuple((a, b) for a in (-1, 0, 1) for b in (-1, 0, 1) if (a, b) != (0, 0))

SUMS = (
    "xp",
    "yp",
    "xq",
    "yq",
    "xpxp",
    "xpyp",
    "ypyp",
    "xqxq",
    "xqyq",
    "yqyq",
    "xpxq",
    "xpyq",
    "ypxq",
    "ypyq",
    "rx",
    "ry",
    "rxxp",
    "rxyp",
    "ryxp",
    "ryyp",
    "rxxq",
    "rxyq",
    "ryxq",
    "ryyq",
)
GROUPS = (
    ("-rxxq", "-rxyq", "-rx", "code", "-ryxq", "-ryyq", "-ry", "0"),
    ("xpxq", "xpyq", "xp", "0", "ypxq", "ypyq", "yp", "0"),
    ("xq", "yq", "n", "0", "xqxq", "xqyq", "yqyq", "0"),
    ("rxxp", "rxyp", "rx", "0", "ryxp", "ryyp", "ry", "0"),
    ("xp", "yp", "n", "0", "xpxp", "xpyp", "ypyp", "0"),
    ("xpxq", "ypxq", "xq", "0", "xpyq", "ypyq", "yq", "0"),
)
TABLE = tuple(name for group in GROUPS for name in group)


def halves(block):
    turned = pltpu.roll(block, 4, 0)
    upper = lax.broadcasted_iota(jnp.int32, (8, NCOLS), 0) < 4
    return jnp.where(upper, block, turned), jnp.where(upper, turned, block)


def row_of(block, upper_row, lower_row):
    upper = lax.broadcasted_iota(jnp.int32, (8, NCOLS), 0) < 4
    one = jnp.broadcast_to(block[upper_row : upper_row + 1], (8, NCOLS))
    two = jnp.broadcast_to(block[lower_row : lower_row + 1], (8, NCOLS))
    return jnp.where(upper, one, two)


def pair_tables(coords_ref, targets_ref, first_ref, second_ref, count_ref, table):
    slots = coords_ref.shape[1]
    pairs = coords_ref.shape[2]
    first = first_ref[...]
    second = second_ref[...]

    def place(index):
        row = lax.shift_right_logical(index, 7)
        section = lax.shift_right_logical(row * 43, 8)
        return section, row - section * ROWS_WIDE, lax.bitwise_and(index, NCOLS - 1)

    near, far = place(first), place(second)
    code = ((far[0] - near[0]) * 16 + far[1] - near[1]) * 16 + far[2] - near[2]
    lines = {"code": code.astype(F32), "n": count_ref[...].astype(F32)}
    squares = jnp.zeros((8, NCOLS), F32)
    for block in range(pairs // NCOLS):
        lanes = pl.ds(block * NCOLS, NCOLS)
        count = jnp.broadcast_to(count_ref[:, lanes], (16, NCOLS))

        def chunk(k, sums):
            rows = pl.ds(pl.multiple_of(k * 16, 16), 16)
            present = lax.broadcasted_iota(jnp.int32, (16, NCOLS), 0) + k * 16 < count

            def load(ref, i):
                return jnp.where(present, ref[i, rows, lanes].astype(F32), 0.0)

            v = {"xp": load(coords_ref, 0), "yp": load(coords_ref, 1), "xq": load(coords_ref, 2)}
            v.update(yq=load(coords_ref, 3), rx=load(targets_ref, 0), ry=load(targets_ref, 1))
            out = []
            for name, total in zip(SUMS, sums):
                term = v[name] if len(name) == 2 else v[name[:2]] * v[name[2:]]
                out.append(total + (term[:8] + term[8:]))
            square = v["rx"] * v["rx"] + v["ry"] * v["ry"]
            out.append(sums[-1] + (square[:8] + square[8:]))
            return tuple(out)

        zero = jnp.zeros((8, NCOLS), F32)
        sums = lax.fori_loop(0, slots // 16, chunk, (zero,) * len(SUMS) + (squares,))
        squares = sums[-1]
        totals = {name: jnp.sum(s, axis=0, keepdims=True) for name, s in zip(SUMS, sums)}
        for row, name in enumerate(TABLE):
            if name == "0":
                line = jnp.zeros((1, NCOLS), F32)
            elif name in lines:
                line = lines[name][:, block * NCOLS : (block + 1) * NCOLS]
            elif name[0] == "-":
                line = -totals[name[1:]]
            else:
                line = totals[name]
            table[row : row + 1, lanes] = line
    return squares


def by_first_tile(first_ref, table, store):
    values = table[...]
    high = values.astype(jnp.bfloat16)
    rest = values - high.astype(F32)
    middle = rest.astype(jnp.bfloat16)
    low = (rest - middle.astype(F32)).astype(jnp.bfloat16)
    parts = jnp.concatenate([high, middle, low], axis=0)
    height, pairs = values.shape
    first = jnp.broadcast_to(first_ref[...], (NCOLS, pairs))
    column = lax.broadcasted_iota(jnp.int32, (NCOLS, pairs), 0)
    for tile_row in range(TILE_ROWS):
        start = ((tile_row // ROWS_DEV + 2) * ROWS_WIDE + tile_row % ROWS_DEV + 2) * NCOLS
        chosen = jnp.where(first == column + start, 1.0, 0.0).astype(jnp.bfloat16)
        moved = lax.dot_general(
            parts, chosen, (((1,), (1,)), ((), ())), preferred_element_type=F32
        )
        moved = moved[:height] + moved[height : 2 * height] + moved[2 * height :]
        for group in range(len(GROUPS)):
            store(group, tile_row, moved[8 * group : 8 * group + 8])


def origin(source):
    block, row = source // TILE_ROWS, lax.rem(source, TILE_ROWS)
    section = (block // 3 - 1) * SEC_DEV + row // ROWS_DEV
    return (section * 256 + (lax.rem(block, 3) - 1) * (ROWS_DEV * 16) + lax.rem(row, ROWS_DEV) * 16)


def target_key(tile_row):
    return float(tile_row // ROWS_DEV * 256 + tile_row % ROWS_DEV * 16)


def kernel(
    sections,
    bands,
    group_one,
    coords_ref,
    targets_ref,
    first_ref,
    second_ref,
    count_ref,
    solution_ref,
    direction_ref,
    table,
    terms,
    moments,
    local,
    keys,
    field,
    sums_one,
    sums_two,
    terms_send,
    terms_recv,
    moments_send,
    moments_recv,
    field_send,
    field_recv,
    sums_send,
    sums_recv,
):
    sec = lax.axis_index("sec")
    band = lax.axis_index("band")
    group_two = sections // group_one * bands

    def neighbour(a, b):
        return (lax.rem(sec + a + sections, sections), lax.rem(band + b + bands, bands))

    def peer_one(d):
        base = sec // group_one * group_one
        return (base + lax.rem(lax.rem(sec, group_one) + d, group_one), band)

    def peer_two(d):
        i = lax.rem(sec // group_one * bands + band + d, group_two)
        return (i // bands * group_one + lax.rem(sec, group_one), lax.rem(i, bands))

    barrier = pltpu.get_barrier_semaphore()
    for a, b in NEIGHBOURS:
        pl.semaphore_signal(barrier, inc=1, device_id=neighbour(a, b), device_id_type=MESH)

    def greet(peer, d, carry):
        pl.semaphore_signal(barrier, inc=1, device_id=peer(d), device_id_type=MESH)
        return carry

    lax.fori_loop(1, group_one, functools.partial(greet, peer_one), 0)
    lax.fori_loop(1, group_two, functools.partial(greet, peer_two), 0)

    squares = pair_tables(coords_ref, targets_ref, first_ref, second_ref, count_ref, table)

    def store(group, tile_row, value):
        if group == 0:
            terms[4, tile_row] = value
        elif group < 3:
            moments[4, group - 1, tile_row] = value
        else:
            local[group - 3, tile_row] = value

    by_first_tile(first_ref, table, store)

    pl.semaphore_wait(barrier, 8 + group_one - 1 + group_two - 1)

    def exchange(buffer, send, recv):
        copies = []
        for i, (a, b) in enumerate(NEIGHBOURS):
            copies.append(
                pltpu.make_async_remote_copy(
                    src_ref=buffer.at[4],
                    dst_ref=buffer.at[(1 - a) * 3 + 1 - b],
                    send_sem=send.at[i],
                    recv_sem=recv.at[i],
                    device_id=neighbour(a, b),
                    device_id_type=MESH,
                )
            )
            copies[-1].start()
        return copies

    terms_copies = exchange(terms, terms_send, terms_recv)
    moments_copies = exchange(moments, moments_send, moments_recv)
    for copy in terms_copies:
        copy.wait_recv()

    zero = jnp.zeros((8, NCOLS), F32)

    def add_terms(source, totals):
        totals = list(totals)
        block, row = source // TILE_ROWS, lax.rem(source, TILE_ROWS)
        value = terms[block, row]
        place = jnp.broadcast_to(value[3:4], (8, NCOLS)) + origin(source).astype(F32)
        for i, shift in enumerate(SHIFTS):
            moved = pltpu.roll(value, shift % NCOLS, 1)
            key = pltpu.roll(place, shift % NCOLS, 1) - float(shift)
            keys[source, i] = key
            for t in range(TILE_ROWS):
                totals[t] = totals[t] + jnp.where(key == target_key(t), moved, 0.0)
        return tuple(totals)

    totals = lax.fori_loop(0, 9 * TILE_ROWS, add_terms, (zero,) * TILE_ROWS)
    held = lax.rem(lax.broadcasted_iota(jnp.int32, (8, NCOLS), 0), 4) < 3
    gradient = []
    for t in range(TILE_ROWS):
        gradient.append(jnp.where(held, totals[t] + local[0, t], 0.0))
        field[4, t] = gradient[t]
    field_copies = exchange(field, field_send, field_recv)

    for copy in moments_copies:
        copy.wait_recv()

    def add_blocks(source, totals):
        totals = list(totals)
        block, row = source // TILE_ROWS, lax.rem(source, TILE_ROWS)
        value = moments[block, 1, row]
        for i, shift in enumerate(SHIFTS):
            moved = pltpu.roll(value, shift % NCOLS, 1)
            key = keys[source, i]
            for t in range(TILE_ROWS):
                totals[t] = totals[t] + jnp.where(key == target_key(t), moved, 0.0)
        return tuple(totals)

    blocks = lax.fori_loop(0, 9 * TILE_ROWS, add_blocks, (zero,) * TILE_ROWS)
    gg = zero
    own = []
    for t in range(TILE_ROWS):
        g = gradient[t]
        gg = gg + g * g
        upper, lower = halves(blocks[t] + local[1, t])
        line = lax.rem(lax.broadcasted_iota(jnp.int32, (8, NCOLS), 0), 4)
        xx, xy, yy = (row_of(lower, k, k) for k in range(3))
        x, y = (row_of(upper, k, k) for k in range(2))
        first = jnp.where(line == 0, xx, jnp.where(line == 1, xy, jnp.where(line == 2, x, 0.0)))
        second = jnp.where(line == 0, xy, jnp.where(line == 1, yy, jnp.where(line == 2, y, 0.0)))
        own.append(first * row_of(g, 0, 4) + second * row_of(g, 1, 5) + upper * row_of(g, 2, 6))

    for copy in field_copies:
        copy.wait_recv()

    def apply(source, carry):
        far, totals = list(carry[:20]), list(carry[20:])
        block, row = source // TILE_ROWS, lax.rem(source, TILE_ROWS)
        g = field[block, row]
        here = origin(source).astype(F32)
        for t in range(TILE_ROWS):
            for i in range(5):
                far[t * 5 + i] = jnp.where(keys[16 + t, i] == here, g, far[t * 5 + i])
        by_a, by_b = halves(moments[block, 0, row])
        by_c, _ = halves(moments[block, 1, row])
        value = by_a * row_of(g, 0, 4) + by_b * row_of(g, 1, 5) + by_c * row_of(g, 2, 6)
        for i, shift in enumerate(SHIFTS):
            moved = pltpu.roll(value, shift % NCOLS, 1)
            key = keys[source, i]
            for t in range(TILE_ROWS):
                totals[t] = totals[t] + jnp.where(key == target_key(t), moved, 0.0)
        return tuple(far) + tuple(totals)

    carry = lax.fori_loop(0, 9 * TILE_ROWS, apply, (zero,) * 24)
    wg, ww = zero, zero
    product = []
    for t in range(TILE_ROWS):
        far = carry[t * 5 + 2]
        for i, shift in enumerate(SHIFTS):
            if shift:
                far = far + pltpu.roll(carry[t * 5 + i], -shift % NCOLS, 1)
        by_a, by_b = halves(local[2, t])
        by_c, _ = halves(local[1, t])
        near = by_a * row_of(far, 0, 4) + by_b * row_of(far, 1, 5) + by_c * row_of(far, 2, 6)
        w = jnp.where(held, own[t] - near - carry[20 + t], 0.0)
        product.append(w)
        wg = wg + w * gradient[t]
        ww = ww + w * w

    lane = lax.broadcasted_iota(jnp.int32, (1, NCOLS), 1)
    line = jnp.zeros((1, NCOLS), F32)
    for k, part in enumerate((squares, gg, wg, ww)):
        total = jnp.sum(jnp.sum(part, axis=0, keepdims=True), axis=1, keepdims=True)
        line = jnp.where(lane == k, total, line)

    def spread_sum(line, buffer, count, peer, i):
        buffer[0:1, :] = line

        def send(d, carry):
            pltpu.make_async_remote_copy(
                src_ref=buffer.at[pl.ds(0, 1), :],
                dst_ref=buffer.at[pl.ds(d, 1), :],
                send_sem=sums_send.at[i],
                recv_sem=sums_recv.at[i],
                device_id=peer(d),
                device_id_type=MESH,
            ).start()
            return carry

        lax.fori_loop(1, count, send, 0)
        others = buffer.at[pl.ds(1, count - 1), :]
        pltpu.make_async_copy(others, others, sums_recv.at[i]).wait()
        return jnp.sum(buffer[0:count, :], axis=0, keepdims=True)

    line = spread_sum(line, sums_one, group_one, peer_one, 0)
    line = spread_sum(line, sums_two, group_two, peer_two, 1)

    def total_of(k):
        return jnp.sum(jnp.where(lane == k, line, 0.0), axis=1, keepdims=True)

    rr, gg, wg, ww = (total_of(k) for k in range(4))
    beta_one = jnp.sqrt(rr)
    norm_g = jnp.sqrt(gg)
    alpha_one = norm_g / beta_one
    beta_two_sq = wg / gg - alpha_one * alpha_one
    beta_two = jnp.sqrt(beta_two_sq)
    on_w = 1.0 / (norm_g * beta_two)
    on_g = -(alpha_one / (beta_one * beta_two) + beta_two / norm_g)
    scaled = on_g / on_w
    alpha_two = on_w * jnp.sqrt(ww + scaled * (2.0 * wg + scaled * gg))
    rho_sq = alpha_one * alpha_one + beta_two_sq
    first_scale = alpha_one * beta_one / (rho_sq * norm_g)
    root = math.sqrt(float(6 * TILE_ROWS * NCOLS * sections * bands))
    scale_w = root * on_w / alpha_two
    scale_g = root * (on_g / alpha_two - beta_two * alpha_two / (rho_sq * norm_g))
    for t in range(TILE_ROWS):
        one = first_scale * gradient[t]
        two = scale_w * product[t] + scale_g * gradient[t]
        for k, row in enumerate((0, 1, 2, 4, 5, 6)):
            solution_ref[k, t : t + 1, :] = one[row : row + 1]
            direction_ref[k, t : t + 1, :] = two[row : row + 1]

    for copies in (terms_copies, moments_copies, field_copies):
        for copy in copies:
            copy.wait_send()
    for buffer, count, i in ((sums_one, group_one, 0), (sums_two, group_two, 1)):
        others = buffer.at[pl.ds(1, count - 1), :]
        pltpu.make_async_copy(others, others, sums_send.at[i]).wait()


def solution(mesh):
    sections, bands = mesh.shape["sec"], mesh.shape["band"]
    group_one = 24 if sections % 24 == 0 else 2
    group_two = sections // group_one * bands

    def on_device(targets, coords, pair_first, pair_second, pair_count):
        slots, pairs = coords.shape[1], coords.shape[-1]
        vmem = pl.BlockSpec(memory_space=pltpu.VMEM)
        shape = (6, TILE_ROWS, NCOLS)
        tile = (8, NCOLS)
        dma = pltpu.SemaphoreType.DMA
        outputs = pl.pallas_call(
            functools.partial(kernel, sections, bands, group_one),
            out_shape=(jax.ShapeDtypeStruct(shape, F32), jax.ShapeDtypeStruct(shape, F32)),
            in_specs=[vmem] * 5,
            out_specs=(vmem, vmem),
            scratch_shapes=[
                pltpu.VMEM((8 * len(GROUPS), pairs), F32),
                pltpu.VMEM((9, TILE_ROWS) + tile, F32),
                pltpu.VMEM((9, 2, TILE_ROWS) + tile, F32),
                pltpu.VMEM((3, TILE_ROWS) + tile, F32),
                pltpu.VMEM((9 * TILE_ROWS, 5) + tile, F32),
                pltpu.VMEM((9, TILE_ROWS) + tile, F32),
                pltpu.VMEM((group_one, NCOLS), F32),
                pltpu.VMEM((group_two, NCOLS), F32),
            ]
            + [dma((8,))] * 6
            + [dma((2,))] * 2,
            compiler_params=pltpu.CompilerParams(
                collective_id=0, has_side_effects=True, vmem_limit_bytes=32 * 2**20
            ),
        )(
            coords.reshape(4, slots, pairs),
            targets.reshape(2, slots, pairs),
            pair_first.reshape(1, pairs),
            pair_second.reshape(1, pairs),
            pair_count.reshape(1, pairs),
        )
        return tuple(o.reshape(6, SEC_DEV, ROWS_DEV, NCOLS) for o in outputs)

    return jax.shard_map(
        on_device,
        mesh=mesh,
        in_specs=(
            P(None, None, "sec", "band", None),
            P(None, None, "sec", "band", None),
            P("sec", "band", None),
            P("sec", "band", None),
            P("sec", "band", None),
        ),
        out_specs=(P(None, "sec", "band", None), P(None, "sec", "band", None)),
        check_vma=False,
    )
```

```python
import functools
import math

import jax
import jax.numpy as jnp
from jax import lax
from jax.experimental import pallas as pl
from jax.experimental.pallas import tpu as pltpu
from jax.sharding import PartitionSpec as P

NCOLS = 128
SEC_DEV = 2
ROWS_DEV = 2
TILE_ROWS = SEC_DEV * ROWS_DEV
ROWS_WIDE = ROWS_DEV + 4
MESH = pl.DeviceIdType.MESH
CHUNKS = 5
F32 = jnp.float32
SHIFTS = (-2, -1, 0, 1, 2)
NEIGHBOURS = ((-1, -1), (1, -1), (-1, 1), (1, 1), (-1, 0), (1, 0), (0, -1), (0, 1))

SUMS = (
    "xp",
    "yp",
    "xq",
    "yq",
    "xpxp",
    "xpyp",
    "ypyp",
    "xqxq",
    "xqyq",
    "yqyq",
    "xpxq",
    "xpyq",
    "ypxq",
    "ypyq",
    "rx",
    "ry",
    "rxxp",
    "rxyp",
    "ryxp",
    "ryyp",
    "rxxq",
    "rxyq",
    "ryxq",
    "ryyq",
)
GROUPS = (
    ("-rxxq", "-rxyq", "-rx", "-ryxq", "-ryyq", "-ry", "0", "0"),
    ("xpxq", "xpyq", "xp", "ypxq", "ypyq", "yp", "code", "0"),
    ("xq", "yq", "n", "xqxq", "xqyq", "yqyq", "0", "0"),
    ("rxxp", "rxyp", "rx", "ryxp", "ryyp", "ry", "0", "0"),
    ("xp", "yp", "n", "xpxp", "xpyp", "ypyp", "0", "0"),
    ("xpxq", "ypxq", "xq", "xpyq", "ypyq", "yq", "0", "0"),
)
TABLE = tuple(name for group in GROUPS for name in group)


def halves(block):
    upper = lax.broadcasted_iota(jnp.int32, (8, NCOLS), 0) < 3
    return jnp.where(upper, block, pltpu.roll(block, 3, 0)), jnp.where(upper, pltpu.roll(block, 5, 0), block)


def row_of(block, upper_row, lower_row):
    upper = lax.broadcasted_iota(jnp.int32, (8, NCOLS), 0) < 3
    one = jnp.broadcast_to(block[upper_row : upper_row + 1], (8, NCOLS))
    two = jnp.broadcast_to(block[lower_row : lower_row + 1], (8, NCOLS))
    return jnp.where(upper, one, two)


def pair_tables(coords_ref, targets_ref, first_ref, second_ref, count_ref, table, ready):
    slots = coords_ref.shape[1]
    pairs = coords_ref.shape[2]
    first = first_ref[...]
    second = second_ref[...]

    def place(index):
        row = lax.shift_right_logical(index, 7)
        section = lax.shift_right_logical(row * 43, 8)
        return section, row - section * ROWS_WIDE, lax.bitwise_and(index, NCOLS - 1)

    near, far = place(first), place(second)
    code = ((far[0] - near[0]) * 16 + far[1] - near[1]) * 16 + far[2] - near[2]
    lines = {"code": code.astype(F32), "n": count_ref[...].astype(F32)}
    squares = jnp.zeros((8, NCOLS), F32)
    for block in range(pairs // NCOLS):
        lanes = pl.ds(block * NCOLS, NCOLS)
        count = jnp.broadcast_to(count_ref[:, lanes], (16, NCOLS))
        ready(block)

        def chunk(k, sums):
            rows = pl.ds(pl.multiple_of(k * 16, 16), 16)
            present = lax.broadcasted_iota(jnp.int32, (16, NCOLS), 0) + k * 16 < count

            def load(ref, i):
                return jnp.where(present, ref[i, rows, lanes].astype(F32), 0.0)

            v = {"xp": load(coords_ref, 0), "yp": load(coords_ref, 1), "xq": load(coords_ref, 2)}
            v.update(yq=load(coords_ref, 3), rx=load(targets_ref, 0), ry=load(targets_ref, 1))
            out = []
            for name, total in zip(SUMS, sums):
                term = v[name] if len(name) == 2 else v[name[:2]] * v[name[2:]]
                out.append(total + (term[:8] + term[8:]))
            square = v["rx"] * v["rx"] + v["ry"] * v["ry"]
            out.append(sums[-1] + (square[:8] + square[8:]))
            return tuple(out)

        def chunks(k, sums):
            for i in range(CHUNKS):
                sums = chunk(k * CHUNKS + i, sums)
            return sums

        zero = jnp.zeros((8, NCOLS), F32)
        sums = (zero,) * len(SUMS) + (squares,)
        sums = lax.fori_loop(0, slots // (16 * CHUNKS), chunks, sums)
        squares = sums[-1]
        totals = {name: jnp.sum(s, axis=0, keepdims=True) for name, s in zip(SUMS, sums)}
        for row, name in enumerate(TABLE):
            if name == "0":
                line = jnp.zeros((1, NCOLS), F32)
            elif name in lines:
                line = lines[name][:, block * NCOLS : (block + 1) * NCOLS]
            elif name[0] == "-":
                line = -totals[name[1:]]
            else:
                line = totals[name]
            table[row : row + 1, lanes] = line
    return squares


def by_first_tile(first_ref, table, store):
    values = table[...]
    high = values.astype(jnp.bfloat16)
    rest = values - high.astype(F32)
    middle = rest.astype(jnp.bfloat16)
    low = (rest - middle.astype(F32)).astype(jnp.bfloat16)
    parts = jnp.concatenate([high, middle, low], axis=0)
    height, pairs = values.shape
    first = jnp.broadcast_to(first_ref[...], (NCOLS, pairs))
    column = lax.broadcasted_iota(jnp.int32, (NCOLS, pairs), 0)
    for tile_row in range(TILE_ROWS):
        start = ((tile_row // ROWS_DEV + 2) * ROWS_WIDE + tile_row % ROWS_DEV + 2) * NCOLS
        chosen = jnp.where(first == column + start, 1.0, 0.0).astype(jnp.bfloat16)
        moved = lax.dot_general(
            parts, chosen, (((1,), (1,)), ((), ())), preferred_element_type=F32
        )
        moved = moved[:height] + moved[height : 2 * height] + moved[2 * height :]
        for group in range(len(GROUPS)):
            store(group, tile_row, moved[8 * group : 8 * group + 8])


def row_key(block, row):
    section, band = block // 3 - 1, block % 3 - 1
    return (section * SEC_DEV + row // ROWS_DEV) * 256 + (band * ROWS_DEV + row % ROWS_DEV) * 16


def dynamic_key(block, row):
    section, band = block // 3 - 1, lax.rem(block, 3) - 1
    key = (section * SEC_DEV + row // ROWS_DEV) * 256 + (band * ROWS_DEV + row % ROWS_DEV) * 16
    return key.astype(F32)


def reach(block, row, target_block, target_row):
    section = (target_block // 3 - block // 3) * SEC_DEV + target_row // 2 - row // 2
    across = (target_block % 3 - block % 3) * ROWS_DEV + target_row % 2 - row % 2
    return abs(section) <= 2 and abs(across) <= 2


def turn(value, shift):
    return pltpu.roll(value, shift % NCOLS, 1) if shift else value


def own_keys(terms, moments, keys, moved):
    for row in range(TILE_ROWS):
        code = jnp.broadcast_to(moments[4, 0, row, 6:7, :], (8, NCOLS)) + float(row_key(4, row))
        for i, shift in enumerate(SHIFTS):
            keys[16 + row, i] = turn(code, shift) - float(shift)
            moved[row, i] = turn(terms[row], shift)


def scatter_to(block, keys, moved, out):
    for target in range(TILE_ROWS):
        total = jnp.zeros((8, NCOLS), F32)
        here = float(row_key(block, target))
        for row in range(TILE_ROWS):
            if reach(4, row, block, target):
                for i in range(5):
                    total = total + jnp.where(keys[16 + row, i] == here, moved[row, i], 0.0)
        out(target, total)


def gather_blocks(moments, keys):
    def step(block, totals):
        totals = list(totals)
        for row in range(TILE_ROWS):
            value = moments[block, 1, row]
            code = jnp.broadcast_to(moments[block, 0, row, 6:7, :], (8, NCOLS))
            code = code + dynamic_key(block, row)
            for i, shift in enumerate(SHIFTS):
                key = turn(code, shift) - float(shift)
                keys[block * TILE_ROWS + row, i] = key
                part = turn(value, shift)
                for t in range(TILE_ROWS):
                    hit = key == float(row_key(4, t))
                    totals[t] = totals[t] + jnp.where(hit, part, 0.0)
        return tuple(totals)

    return lax.fori_loop(0, 9, step, (jnp.zeros((8, NCOLS), F32),) * TILE_ROWS)


def own_blocks(block, g):
    upper, lower = halves(block)
    line = lax.rem(lax.broadcasted_iota(jnp.int32, (8, NCOLS), 0), 3)
    xx, xy, yy = (row_of(lower, k, k) for k in range(3))
    x, y = (row_of(upper, k, k) for k in range(2))
    first = jnp.where(line == 0, xx, jnp.where(line == 1, xy, jnp.where(line == 2, x, 0.0)))
    second = jnp.where(line == 0, xy, jnp.where(line == 1, yy, jnp.where(line == 2, y, 0.0)))
    return first * row_of(g, 0, 3) + second * row_of(g, 1, 4) + upper * row_of(g, 2, 5)


def apply_pairs(field, moments, local, keys):
    def step(block, carry):
        far, totals = list(carry[:20]), list(carry[20:])
        for row in range(TILE_ROWS):
            g = field[block, row]
            here = dynamic_key(block, row)
            for t in range(TILE_ROWS):
                for i in range(5):
                    far[t * 5 + i] = jnp.where(keys[16 + t, i] == here, g, far[t * 5 + i])
            by_a, by_b = halves(moments[block, 0, row])
            by_c, _ = halves(moments[block, 1, row])
            value = by_a * row_of(g, 0, 3) + by_b * row_of(g, 1, 4) + by_c * row_of(g, 2, 5)
            for i, shift in enumerate(SHIFTS):
                part = turn(value, shift)
                key = keys[block * TILE_ROWS + row, i]
                for t in range(TILE_ROWS):
                    hit = key == float(row_key(4, t))
                    totals[t] = totals[t] + jnp.where(hit, part, 0.0)
        return tuple(far) + tuple(totals)

    carry = lax.fori_loop(0, 9, step, (jnp.zeros((8, NCOLS), F32),) * 24)
    out = []
    for t in range(TILE_ROWS):
        far = carry[t * 5 + 2]
        for i, shift in enumerate(SHIFTS):
            if shift:
                far = far + turn(carry[t * 5 + i], -shift)
        by_a, by_b = halves(local[2, t])
        by_c, _ = halves(local[1, t])
        near = by_a * row_of(far, 0, 3) + by_b * row_of(far, 1, 4) + by_c * row_of(far, 2, 5)
        out.append(near + carry[20 + t])
    return out


def kernel(
    sections,
    bands,
    group_one,
    coords_ref,
    targets_ref,
    first_ref,
    second_ref,
    count_ref,
    solution_ref,
    direction_ref,
    coords,
    targets,
    first,
    second,
    count,
    table,
    terms,
    folded,
    arrived,
    moments,
    local,
    keys,
    moved,
    field,
    sums_one,
    sums_two,
    load_sems,
    terms_send,
    terms_recv,
    moments_send,
    moments_recv,
    field_send,
    field_recv,
    sums_send,
    sums_recv,
):
    sec = lax.axis_index("sec")
    band = lax.axis_index("band")
    group_two = sections // group_one * bands

    def neighbour(a, b):
        return (lax.rem(sec + a + sections, sections), lax.rem(band + b + bands, bands))

    def peer_one(d):
        base = sec // group_one * group_one
        return (base + lax.rem(lax.rem(sec, group_one) + d, group_one), band)

    def peer_two(d):
        i = lax.rem(sec // group_one * bands + band + d, group_two)
        return (i // bands * group_one + lax.rem(sec, group_one), lax.rem(i, bands))

    barrier = pltpu.get_barrier_semaphore()
    for a, b in NEIGHBOURS:
        pl.semaphore_signal(barrier, inc=1, device_id=neighbour(a, b), device_id_type=MESH)

    def greet(peer, d, carry):
        pl.semaphore_signal(barrier, inc=1, device_id=peer(d), device_id_type=MESH)
        return carry

    lax.fori_loop(1, group_one, functools.partial(greet, peer_one), 0)
    lax.fori_loop(1, group_two, functools.partial(greet, peer_two), 0)

    loads = []

    def load(source, target):
        loads.append(pltpu.make_async_copy(source, target, load_sems.at[len(loads)]))
        loads[-1].start()

    load(count_ref, count)
    load(first_ref, first)
    load(second_ref, second)
    blocks = coords_ref.shape[2] // NCOLS
    for i in range(blocks):
        lanes = pl.ds(i * NCOLS, NCOLS)
        load(coords_ref.at[:, :, lanes], coords.at[:, :, lanes])
        load(targets_ref.at[:, :, lanes], targets.at[:, :, lanes])
    for copy in loads[:3]:
        copy.wait()

    def ready(i):
        loads[3 + 2 * i].wait()
        loads[4 + 2 * i].wait()

    squares = pair_tables(coords, targets, first, second, count, table, ready)

    def store(group, tile_row, value):
        if group == 0:
            terms[tile_row] = value
        elif group < 3:
            moments[4, group - 1, tile_row] = value
        else:
            local[group - 3, tile_row] = value

    by_first_tile(first, table, store)
    own_keys(terms, moments, keys, moved)

    pl.semaphore_wait(barrier, 8 + group_one - 1 + group_two - 1)

    def send(source, target, send_sem, recv_sem, i, part=lambda ref: ref.at[:, 0:6]):
        a, b = NEIGHBOURS[i]
        copy = pltpu.make_async_remote_copy(
            src_ref=source,
            dst_ref=part(target.at[(1 - a) * 3 + 1 - b]),
            send_sem=send_sem.at[i],
            recv_sem=recv_sem.at[i],
            device_id=neighbour(a, b),
            device_id_type=MESH,
        )
        copy.start()
        return copy

    terms_copies = []
    for i, (a, b) in enumerate(NEIGHBOURS):
        block = (a + 1) * 3 + b + 1

        def put(t, value, block=block):
            folded[block, t] = value

        scatter_to(block, keys, moved, put)
        terms_copies.append(send(folded.at[block, :, 0:6], arrived, terms_send, terms_recv, i))
    moments_copies = []
    for i in range(8):
        moments_copies.append(send(moments.at[4], moments, moments_send, moments_recv, i, lambda ref: ref))

    gradient = [None] * TILE_ROWS

    def keep(t, value):
        gradient[t] = value + local[0, t]

    scatter_to(4, keys, moved, keep)
    for i, (a, b) in enumerate(NEIGHBOURS):
        terms_copies[i].wait_recv()
        for t in range(TILE_ROWS):
            gradient[t] = gradient[t] + arrived[(1 - a) * 3 + 1 - b, t]
    held = lax.broadcasted_iota(jnp.int32, (8, NCOLS), 0) < 6
    for t in range(TILE_ROWS):
        gradient[t] = jnp.where(held, gradient[t], 0.0)
        field[4, t] = gradient[t]
    field_copies = []
    for i in range(8):
        field_copies.append(send(field.at[4, :, 0:6], field, field_send, field_recv, i))

    for copy in moments_copies:
        copy.wait_recv()
    zero = jnp.zeros((8, NCOLS), F32)
    gg = zero
    own = []
    for t, block in enumerate(gather_blocks(moments, keys)):
        gg = gg + gradient[t] * gradient[t]
        own.append(own_blocks(block + local[1, t], gradient[t]))

    for copy in field_copies:
        copy.wait_recv()
    others = apply_pairs(field, moments, local, keys)
    wg, ww = zero, zero
    product = []
    for t in range(TILE_ROWS):
        w = jnp.where(held, own[t] - others[t], 0.0)
        product.append(w)
        wg = wg + w * gradient[t]
        ww = ww + w * w

    lane = lax.broadcasted_iota(jnp.int32, (1, NCOLS), 1)
    line = jnp.zeros((1, NCOLS), F32)
    for k, part in enumerate((squares, gg, wg, ww)):
        total = jnp.sum(jnp.sum(part, axis=0, keepdims=True), axis=1, keepdims=True)
        line = jnp.where(lane == k, total, line)

    def spread_sum(line, buffer, count, peer, i):
        buffer[0:1, :] = line

        def send_to(k, carry):
            step = k // 2
            d = count // 2 + (2 * lax.rem(k, 2) - 1) * step
            pltpu.make_async_remote_copy(
                src_ref=buffer.at[pl.ds(0, 1), :],
                dst_ref=buffer.at[pl.ds(d, 1), :],
                send_sem=sums_send.at[i],
                recv_sem=sums_recv.at[i],
                device_id=peer(d),
                device_id_type=MESH,
            ).start()
            return carry

        lax.fori_loop(1, count, send_to, 0)
        others = buffer.at[pl.ds(1, count - 1), :]
        pltpu.make_async_copy(others, others, sums_recv.at[i]).wait()
        return jnp.sum(buffer[0:count, :], axis=0, keepdims=True)

    line = spread_sum(line, sums_one, group_one, peer_one, 0)
    line = spread_sum(line, sums_two, group_two, peer_two, 1)

    def total_of(k):
        return jnp.sum(jnp.where(lane == k, line, 0.0), axis=1, keepdims=True)

    rr, gg, wg, ww = (total_of(k) for k in range(4))
    beta_one = jnp.sqrt(rr)
    norm_g = jnp.sqrt(gg)
    alpha_one = norm_g / beta_one
    beta_two_sq = wg / gg - alpha_one * alpha_one
    beta_two = jnp.sqrt(beta_two_sq)
    on_w = 1.0 / (norm_g * beta_two)
    on_g = -(alpha_one / (beta_one * beta_two) + beta_two / norm_g)
    scaled = on_g / on_w
    alpha_two = on_w * jnp.sqrt(ww + scaled * (2.0 * wg + scaled * gg))
    rho_sq = alpha_one * alpha_one + beta_two_sq
    first_scale = alpha_one * beta_one / (rho_sq * norm_g)
    root = math.sqrt(float(6 * TILE_ROWS * NCOLS * sections * bands))
    scale_w = root * on_w / alpha_two
    scale_g = root * (on_g / alpha_two - beta_two * alpha_two / (rho_sq * norm_g))
    for t in range(TILE_ROWS):
        one = first_scale * gradient[t]
        two = scale_w * product[t] + scale_g * gradient[t]
        for k, row in enumerate(range(6)):
            solution_ref[k, t : t + 1, :] = one[row : row + 1]
            direction_ref[k, t : t + 1, :] = two[row : row + 1]

    for copies in (terms_copies, moments_copies, field_copies):
        for copy in copies:
            copy.wait_send()
    for buffer, count, i in ((sums_one, group_one, 0), (sums_two, group_two, 1)):
        others = buffer.at[pl.ds(1, count - 1), :]
        pltpu.make_async_copy(others, others, sums_send.at[i]).wait()


def solution(mesh):
    sections, bands = mesh.shape["sec"], mesh.shape["band"]
    group_one = 24 if sections % 24 == 0 else 2
    group_two = sections // group_one * bands

    def on_device(targets, coords, pair_first, pair_second, pair_count):
        slots, pairs = coords.shape[1], coords.shape[-1]
        vmem = pl.BlockSpec(memory_space=pltpu.VMEM)
        anywhere = pl.BlockSpec(memory_space=pl.ANY)
        shape = (6, TILE_ROWS, NCOLS)
        tile = (8, NCOLS)
        dma = pltpu.SemaphoreType.DMA
        outputs = pl.pallas_call(
            functools.partial(kernel, sections, bands, group_one),
            out_shape=(jax.ShapeDtypeStruct(shape, F32), jax.ShapeDtypeStruct(shape, F32)),
            in_specs=[anywhere] * 5,
            out_specs=(vmem, vmem),
            scratch_shapes=[
                pltpu.VMEM((4, slots, pairs), coords.dtype),
                pltpu.VMEM((2, slots, pairs), targets.dtype),
                pltpu.VMEM((1, pairs), jnp.int32),
                pltpu.VMEM((1, pairs), jnp.int32),
                pltpu.VMEM((1, pairs), jnp.int32),
                pltpu.VMEM((8 * len(GROUPS), pairs), F32),
                pltpu.VMEM((TILE_ROWS,) + tile, F32),
                pltpu.VMEM((9, TILE_ROWS) + tile, F32),
                pltpu.VMEM((9, TILE_ROWS) + tile, F32),
                pltpu.VMEM((9, 2, TILE_ROWS) + tile, F32),
                pltpu.VMEM((3, TILE_ROWS) + tile, F32),
                pltpu.VMEM((9 * TILE_ROWS, 5) + tile, F32),
                pltpu.VMEM((TILE_ROWS, 5) + tile, F32),
                pltpu.VMEM((9, TILE_ROWS) + tile, F32),
                pltpu.VMEM((group_one, NCOLS), F32),
                pltpu.VMEM((group_two, NCOLS), F32),
            ]
            + [dma((3 + 2 * (pairs // NCOLS),))]
            + [dma((8,))] * 6
            + [dma((2,))] * 2,
            compiler_params=pltpu.CompilerParams(
                collective_id=0, has_side_effects=True, vmem_limit_bytes=60 * 2**20
            ),
        )(
            coords.reshape(4, slots, pairs),
            targets.reshape(2, slots, pairs),
            pair_first.reshape(1, pairs),
            pair_second.reshape(1, pairs),
            pair_count.reshape(1, pairs),
        )
        return tuple(o.reshape(6, SEC_DEV, ROWS_DEV, NCOLS) for o in outputs)

    return jax.shard_map(
        on_device,
        mesh=mesh,
        in_specs=(
            P(None, None, "sec", "band", None),
            P(None, None, "sec", "band", None),
            P("sec", "band", None),
            P("sec", "band", None),
            P("sec", "band", None),
        ),
        out_specs=(P(None, "sec", "band", None), P(None, "sec", "band", None)),
        check_vma=False,
    )
```

```python
import functools
import math

import jax
import jax.numpy as jnp
from jax import lax
from jax.experimental import pallas as pl
from jax.experimental.pallas import tpu as pltpu
from jax.sharding import PartitionSpec as P

NCOLS = 128
SEC_DEV = 2
ROWS_DEV = 2
TILE_ROWS = SEC_DEV * ROWS_DEV
ROWS_WIDE = ROWS_DEV + 4
MESH = pl.DeviceIdType.MESH
CHUNKS = 5
VMEM_BYTES = 56426496
F32 = jnp.float32
SHIFTS = (-2, -1, 0, 1, 2)
EDGES = (1, 3, 5, 7)
CORNERS = (0, 2, 6, 8)
NEIGHBOURS = ((-1, 0), (1, 0), (0, -1), (0, 1), (-1, -1), (1, -1), (-1, 1), (1, 1))

SUMS = (
    "xp",
    "yp",
    "xq",
    "yq",
    "xpxp",
    "xpyp",
    "ypyp",
    "xqxq",
    "xqyq",
    "yqyq",
    "xpxq",
    "xpyq",
    "ypxq",
    "ypyq",
    "rx",
    "ry",
    "rxxp",
    "rxyp",
    "ryxp",
    "ryyp",
    "rxxq",
    "rxyq",
    "ryxq",
    "ryyq",
)
GROUPS = (
    ("-rxxq", "-rxyq", "-rx", "-ryxq", "-ryyq", "-ry", "0", "0"),
    ("xpxq", "xpyq", "xp", "ypxq", "ypyq", "yp", "code", "0"),
    ("xq", "yq", "n", "xqxq", "xqyq", "yqyq", "0", "0"),
    ("rxxp", "rxyp", "rx", "ryxp", "ryyp", "ry", "0", "0"),
    ("xp", "yp", "n", "xpxp", "xpyp", "ypyp", "0", "0"),
    ("xpxq", "ypxq", "xq", "xpyq", "ypyq", "yq", "0", "0"),
)
TABLE = tuple(name for group in GROUPS for name in group)


def halves(block):
    upper = lax.broadcasted_iota(jnp.int32, (8, NCOLS), 0) < 3
    return jnp.where(upper, block, pltpu.roll(block, 3, 0)), jnp.where(upper, pltpu.roll(block, 5, 0), block)


def row_of(block, upper_row, lower_row):
    upper = lax.broadcasted_iota(jnp.int32, (8, NCOLS), 0) < 3
    one = jnp.broadcast_to(block[upper_row : upper_row + 1], (8, NCOLS))
    two = jnp.broadcast_to(block[lower_row : lower_row + 1], (8, NCOLS))
    return jnp.where(upper, one, two)


def pair_tables(coords_ref, targets_ref, first_ref, second_ref, count_ref, table, ready):
    slots = coords_ref.shape[1]
    pairs = coords_ref.shape[2]
    first = first_ref[...]
    second = second_ref[...]

    def place(index):
        row = lax.shift_right_logical(index, 7)
        section = lax.shift_right_logical(row * 43, 8)
        return section, row - section * ROWS_WIDE, lax.bitwise_and(index, NCOLS - 1)

    near, far = place(first), place(second)
    code = ((far[0] - near[0]) * 16 + far[1] - near[1]) * 16 + far[2] - near[2]
    lines = {"code": code.astype(F32), "n": count_ref[...].astype(F32)}
    squares = jnp.zeros((8, NCOLS), F32)
    for block in range(pairs // NCOLS):
        lanes = pl.ds(block * NCOLS, NCOLS)
        count = jnp.broadcast_to(count_ref[:, lanes], (16, NCOLS))
        ready(block)

        def chunk(k, sums):
            rows = pl.ds(pl.multiple_of(k * 16, 16), 16)
            present = lax.broadcasted_iota(jnp.int32, (16, NCOLS), 0) + k * 16 < count

            def load(ref, i):
                return jnp.where(present, ref[i, rows, lanes].astype(F32), 0.0)

            v = {"xp": load(coords_ref, 0), "yp": load(coords_ref, 1), "xq": load(coords_ref, 2)}
            v.update(yq=load(coords_ref, 3), rx=load(targets_ref, 0), ry=load(targets_ref, 1))
            out = []
            for name, total in zip(SUMS, sums):
                term = v[name] if len(name) == 2 else v[name[:2]] * v[name[2:]]
                out.append(total + (term[:8] + term[8:]))
            square = v["rx"] * v["rx"] + v["ry"] * v["ry"]
            out.append(sums[-1] + (square[:8] + square[8:]))
            return tuple(out)

        def chunks(k, sums):
            for i in range(CHUNKS):
                sums = chunk(k * CHUNKS + i, sums)
            return sums

        zero = jnp.zeros((8, NCOLS), F32)
        sums = (zero,) * len(SUMS) + (squares,)
        sums = lax.fori_loop(0, slots // (16 * CHUNKS), chunks, sums)
        squares = sums[-1]
        totals = {name: jnp.sum(s, axis=0, keepdims=True) for name, s in zip(SUMS, sums)}
        for row, name in enumerate(TABLE):
            if name == "0":
                line = jnp.zeros((1, NCOLS), F32)
            elif name in lines:
                line = lines[name][:, block * NCOLS : (block + 1) * NCOLS]
            elif name[0] == "-":
                line = -totals[name[1:]]
            else:
                line = totals[name]
            table[row : row + 1, lanes] = line
    return squares


def place_table(first_ref, chosen):
    pairs = first_ref.shape[1]
    first = jnp.broadcast_to(first_ref[...], (NCOLS, pairs))
    column = lax.broadcasted_iota(jnp.int32, (NCOLS, pairs), 0)
    for row in range(TILE_ROWS):
        start = ((row // ROWS_DEV + 2) * ROWS_WIDE + row % ROWS_DEV + 2) * NCOLS
        chosen[row] = jnp.where(first == column + start, 1.0, 0.0).astype(jnp.bfloat16)


def by_first_tile(chosen, table, store):
    values = table[...]
    high = values.astype(jnp.bfloat16)
    rest = values - high.astype(F32)
    middle = rest.astype(jnp.bfloat16)
    low = (rest - middle.astype(F32)).astype(jnp.bfloat16)
    parts = jnp.concatenate([high, middle, low], axis=0)
    height = values.shape[0]
    for row in range(TILE_ROWS):
        moved = lax.dot_general(
            parts, chosen[row], (((1,), (1,)), ((), ())), preferred_element_type=F32
        )
        moved = moved[:height] + moved[height : 2 * height] + moved[2 * height :]
        for group in range(len(GROUPS)):
            store(group, row, moved[8 * group : 8 * group + 8])


def row_key(block, row):
    section, band = block // 3 - 1, block % 3 - 1
    return (section * SEC_DEV + row // ROWS_DEV) * 256 + (band * ROWS_DEV + row % ROWS_DEV) * 16


def dynamic_key(block, row):
    section, band = block // 3 - 1, lax.rem(block, 3) - 1
    key = (section * SEC_DEV + row // ROWS_DEV) * 256 + (band * ROWS_DEV + row % ROWS_DEV) * 16
    return key.astype(F32)


def reach(block, row, target_block, target_row):
    section = (target_block // 3 - block // 3) * SEC_DEV + target_row // 2 - row // 2
    across = (target_block % 3 - block % 3) * ROWS_DEV + target_row % 2 - row % 2
    return abs(section) <= 2 and abs(across) <= 2


def turn(value, shift):
    return pltpu.roll(value, shift % NCOLS, 1) if shift else value


def own_keys(terms, moments, keys, moved):
    for row in range(TILE_ROWS):
        code = jnp.broadcast_to(moments[4, 0, row, 6:7, :], (8, NCOLS)) + float(row_key(4, row))
        for i, shift in enumerate(SHIFTS):
            keys[16 + row, i] = turn(code, shift) - float(shift)
            moved[row, i] = turn(terms[row], shift)


def scatter_to(block, keys, moved, out):
    for target in range(TILE_ROWS):
        total = jnp.zeros((8, NCOLS), F32)
        here = float(row_key(block, target))
        for row in range(TILE_ROWS):
            if reach(4, row, block, target):
                for i in range(5):
                    total = total + jnp.where(keys[16 + row, i] == here, moved[row, i], 0.0)
        out(target, total)


def gather_blocks(moments, keys):
    def step(block, totals):
        totals = list(totals)
        for row in range(TILE_ROWS):
            value = moments[block, 1, row]
            code = jnp.broadcast_to(moments[block, 0, row, 6:7, :], (8, NCOLS))
            code = code + dynamic_key(block, row)
            for i, shift in enumerate(SHIFTS):
                key = turn(code, shift) - float(shift)
                keys[block * TILE_ROWS + row, i] = key
                part = turn(value, shift)
                for t in range(TILE_ROWS):
                    hit = key == float(row_key(4, t))
                    totals[t] = totals[t] + jnp.where(hit, part, 0.0)
        return tuple(totals)

    return lax.fori_loop(0, 9, step, (jnp.zeros((8, NCOLS), F32),) * TILE_ROWS)


def own_blocks(block, g):
    upper, lower = halves(block)
    line = lax.rem(lax.broadcasted_iota(jnp.int32, (8, NCOLS), 0), 3)
    xx, xy, yy = (row_of(lower, k, k) for k in range(3))
    x, y = (row_of(upper, k, k) for k in range(2))
    first = jnp.where(line == 0, xx, jnp.where(line == 1, xy, jnp.where(line == 2, x, 0.0)))
    second = jnp.where(line == 0, xy, jnp.where(line == 1, yy, jnp.where(line == 2, y, 0.0)))
    return first * row_of(g, 0, 3) + second * row_of(g, 1, 4) + upper * row_of(g, 2, 5)


def apply_pairs(field, moments, local, keys, landed):
    def step(block, carry):
        far, totals = list(carry[:20]), list(carry[20:])
        for row in range(TILE_ROWS):
            g = field[block, row]
            here = dynamic_key(block, row)
            for t in range(TILE_ROWS):
                for i in range(5):
                    far[t * 5 + i] = jnp.where(keys[16 + t, i] == here, g, far[t * 5 + i])
            by_a, by_b = halves(moments[block, 0, row])
            by_c, _ = halves(moments[block, 1, row])
            value = by_a * row_of(g, 0, 3) + by_b * row_of(g, 1, 4) + by_c * row_of(g, 2, 5)
            for i, shift in enumerate(SHIFTS):
                part = turn(value, shift)
                key = keys[block * TILE_ROWS + row, i]
                for t in range(TILE_ROWS):
                    hit = key == float(row_key(4, t))
                    totals[t] = totals[t] + jnp.where(hit, part, 0.0)
        return tuple(far) + tuple(totals)

    def edge(k, carry):
        landed(2 * k + 1)
        return step(2 * k + 1, carry)

    def corner(k, carry):
        block = 2 * k + 2 * (k // 2)
        landed(block)
        return step(block, carry)

    carry = step(jnp.int32(4), (jnp.zeros((8, NCOLS), F32),) * 24)
    carry = lax.fori_loop(0, len(EDGES), edge, carry)
    carry = lax.fori_loop(0, len(CORNERS), corner, carry)
    out = []
    for t in range(TILE_ROWS):
        far = carry[t * 5 + 2]
        for i, shift in enumerate(SHIFTS):
            if shift:
                far = far + turn(carry[t * 5 + i], -shift)
        by_a, by_b = halves(local[2, t])
        by_c, _ = halves(local[1, t])
        near = by_a * row_of(far, 0, 3) + by_b * row_of(far, 1, 4) + by_c * row_of(far, 2, 5)
        out.append(near + carry[20 + t])
    return out


def kernel(
    sections,
    bands,
    group_one,
    coords_ref,
    targets_ref,
    first_ref,
    second_ref,
    count_ref,
    gradient_ref,
    product_ref,
    solution_scale_ref,
    product_scale_ref,
    gradient_scale_ref,
    coords,
    targets,
    first,
    second,
    count,
    chosen,
    table,
    terms,
    folded,
    arrived,
    moments,
    local,
    keys,
    moved,
    field,
    sums_one,
    sums_two,
    load_sems,
    terms_send,
    terms_recv,
    moments_send,
    moments_recv,
    field_send,
    field_recv,
    sums_send,
    sums_recv,
):
    sec = lax.axis_index("sec")
    band = lax.axis_index("band")
    group_two = sections // group_one * bands

    def neighbour(a, b):
        return (lax.rem(sec + a + sections, sections), lax.rem(band + b + bands, bands))

    def peer_one(d):
        base = sec // group_one * group_one
        return (base + lax.rem(lax.rem(sec, group_one) + d, group_one), band)

    def peer_two(d):
        i = lax.rem(sec // group_one * bands + band + d, group_two)
        return (i // bands * group_one + lax.rem(sec, group_one), lax.rem(i, bands))

    barrier = pltpu.get_barrier_semaphore()
    for a, b in NEIGHBOURS:
        pl.semaphore_signal(barrier, inc=1, device_id=neighbour(a, b), device_id_type=MESH)

    def greet(peer, d, carry):
        pl.semaphore_signal(barrier, inc=1, device_id=peer(d), device_id_type=MESH)
        return carry

    lax.fori_loop(1, group_one, functools.partial(greet, peer_one), 0)
    lax.fori_loop(1, group_two, functools.partial(greet, peer_two), 0)

    loads = []

    def load(source, target):
        loads.append(pltpu.make_async_copy(source, target, load_sems.at[len(loads)]))
        loads[-1].start()

    load(count_ref, count)
    load(first_ref, first)
    load(second_ref, second)
    blocks = coords_ref.shape[2] // NCOLS
    for i in range(blocks):
        lanes = pl.ds(i * NCOLS, NCOLS)
        load(coords_ref.at[:, :, lanes], coords.at[:, :, lanes])
        load(targets_ref.at[:, :, lanes], targets.at[:, :, lanes])
    for copy in loads[:3]:
        copy.wait()
    place_table(first, chosen)

    def ready(i):
        loads[3 + 2 * i].wait()
        loads[4 + 2 * i].wait()

    squares = pair_tables(coords, targets, first, second, count, table, ready)

    def store(group, tile_row, value):
        if group == 0:
            terms[tile_row] = value
        elif group < 3:
            moments[4, group - 1, tile_row] = value
        else:
            local[group - 3, tile_row] = value

    by_first_tile(chosen, table, store)
    own_keys(terms, moments, keys, moved)

    pl.semaphore_wait(barrier, 8 + group_one - 1 + group_two - 1)

    def send(source, target, send_sem, recv_sem, i, part=lambda ref: ref.at[:, 0:6]):
        a, b = NEIGHBOURS[i]
        copy = pltpu.make_async_remote_copy(
            src_ref=source,
            dst_ref=part(target.at[(1 - a) * 3 + 1 - b]),
            send_sem=send_sem.at[i],
            recv_sem=recv_sem.at[(1 - a) * 3 + 1 - b],
            device_id=neighbour(a, b),
            device_id_type=MESH,
        )
        copy.start()
        return copy

    def landed(ref, sem):
        pltpu.make_async_copy(ref, ref, sem).wait()

    terms_copies = []
    for i, (a, b) in enumerate(NEIGHBOURS):
        block = (a + 1) * 3 + b + 1

        def put(t, value, block=block):
            folded[block, t] = value

        scatter_to(block, keys, moved, put)
        terms_copies.append(send(folded.at[block, :, 0:6], arrived, terms_send, terms_recv, i))
    moments_copies = []
    for i in range(8):
        moments_copies.append(send(moments.at[4], moments, moments_send, moments_recv, i, lambda ref: ref))

    gradient = [None] * TILE_ROWS

    def keep(t, value):
        gradient[t] = value + local[0, t]

    scatter_to(4, keys, moved, keep)
    for block in EDGES + CORNERS:
        landed(arrived.at[block, :, 0:6], terms_recv.at[block])
        for t in range(TILE_ROWS):
            gradient[t] = gradient[t] + arrived[block, t]
    held = lax.broadcasted_iota(jnp.int32, (8, NCOLS), 0) < 6
    for t in range(TILE_ROWS):
        gradient[t] = jnp.where(held, gradient[t], 0.0)
        field[4, t] = gradient[t]
    field_copies = []
    for i in range(8):
        field_copies.append(send(field.at[4, :, 0:6], field, field_send, field_recv, i))

    for block in EDGES + CORNERS:
        landed(moments.at[block], moments_recv.at[block])
    zero = jnp.zeros((8, NCOLS), F32)
    gg = zero
    own = []
    for t, block in enumerate(gather_blocks(moments, keys)):
        gg = gg + gradient[t] * gradient[t]
        own.append(own_blocks(block + local[1, t], gradient[t]))

    def field_landed(block):
        landed(field.at[block, :, 0:6], field_recv.at[block])

    others = apply_pairs(field, moments, local, keys, field_landed)
    wg, ww = zero, zero
    product = []
    for t in range(TILE_ROWS):
        w = jnp.where(held, own[t] - others[t], 0.0)
        product.append(w)
        wg = wg + w * gradient[t]
        ww = ww + w * w

    for t in range(TILE_ROWS):
        for k in range(6):
            gradient_ref[k, t : t + 1, :] = gradient[t][k : k + 1]
            product_ref[k, t : t + 1, :] = product[t][k : k + 1]

    lane = lax.broadcasted_iota(jnp.int32, (1, NCOLS), 1)
    line = jnp.zeros((1, NCOLS), F32)
    for k, part in enumerate((squares, gg, wg, ww)):
        total = jnp.sum(jnp.sum(part, axis=0, keepdims=True), axis=1, keepdims=True)
        line = jnp.where(lane == k, total, line)

    def spread_sum(line, buffer, count, peer, i):
        buffer[0:1, :] = line

        def send_to(k, carry):
            step = k // 2
            d = count // 2 + (2 * lax.rem(k, 2) - 1) * step
            pltpu.make_async_remote_copy(
                src_ref=buffer.at[pl.ds(0, 1), :],
                dst_ref=buffer.at[pl.ds(d, 1), :],
                send_sem=sums_send.at[i],
                recv_sem=sums_recv.at[i],
                device_id=peer(d),
                device_id_type=MESH,
            ).start()
            return carry

        lax.fori_loop(1, count, send_to, 0)
        others = buffer.at[pl.ds(1, count - 1), :]
        pltpu.make_async_copy(others, others, sums_recv.at[i]).wait()
        return jnp.sum(buffer[0:count, :], axis=0, keepdims=True)

    line = spread_sum(line, sums_one, group_one, peer_one, 0)
    line = spread_sum(line, sums_two, group_two, peer_two, 1)

    rr, gg, wg, ww = (jnp.broadcast_to(line[:, k : k + 1], (1, NCOLS)) for k in range(4))
    beta_one = jnp.sqrt(rr)
    norm_g = jnp.sqrt(gg)
    alpha_one = norm_g / beta_one
    beta_two_sq = wg / gg - alpha_one * alpha_one
    beta_two = jnp.sqrt(beta_two_sq)
    on_w = 1.0 / (norm_g * beta_two)
    on_g = -(alpha_one / (beta_one * beta_two) + beta_two / norm_g)
    scaled = on_g / on_w
    alpha_two = on_w * jnp.sqrt(ww + scaled * (2.0 * wg + scaled * gg))
    rho_sq = alpha_one * alpha_one + beta_two_sq
    first_scale = alpha_one * beta_one / (rho_sq * norm_g)
    root = math.sqrt(float(6 * TILE_ROWS * NCOLS * sections * bands))
    scale_w = root * on_w / alpha_two
    scale_g = root * (on_g / alpha_two - beta_two * alpha_two / (rho_sq * norm_g))
    solution_scale_ref[...] = first_scale
    product_scale_ref[...] = scale_w
    gradient_scale_ref[...] = scale_g

    for copies in (terms_copies, moments_copies, field_copies):
        for copy in copies:
            copy.wait_send()
    for buffer, count, i in ((sums_one, group_one, 0), (sums_two, group_two, 1)):
        others = buffer.at[pl.ds(1, count - 1), :]
        pltpu.make_async_copy(others, others, sums_send.at[i]).wait()


def solution(mesh):
    sections, bands = mesh.shape["sec"], mesh.shape["band"]
    group_one = 24 if sections % 24 == 0 else 2
    group_two = sections // group_one * bands

    def on_device(targets, coords, pair_first, pair_second, pair_count):
        slots, pairs = coords.shape[1], coords.shape[-1]
        vmem = pl.BlockSpec(memory_space=pltpu.VMEM)
        anywhere = pl.BlockSpec(memory_space=pl.ANY)
        shape = (6, TILE_ROWS, NCOLS)
        tile = (8, NCOLS)
        dma = pltpu.SemaphoreType.DMA
        gradient, product, *scales = pl.pallas_call(
            functools.partial(kernel, sections, bands, group_one),
            out_shape=tuple(jax.ShapeDtypeStruct(s, F32) for s in (shape, shape) + ((1, NCOLS),) * 3),
            in_specs=[anywhere] * 5,
            out_specs=(vmem,) * 5,
            scratch_shapes=[
                pltpu.VMEM((4, slots, pairs), coords.dtype),
                pltpu.VMEM((2, slots, pairs), targets.dtype),
                pltpu.VMEM((1, pairs), jnp.int32),
                pltpu.VMEM((1, pairs), jnp.int32),
                pltpu.VMEM((1, pairs), jnp.int32),
                pltpu.VMEM((TILE_ROWS, NCOLS, pairs), jnp.bfloat16),
                pltpu.VMEM((8 * len(GROUPS), pairs), F32),
                pltpu.VMEM((TILE_ROWS,) + tile, F32),
                pltpu.VMEM((9, TILE_ROWS) + tile, F32),
                pltpu.VMEM((9, TILE_ROWS) + tile, F32),
                pltpu.VMEM((9, 2, TILE_ROWS) + tile, F32),
                pltpu.VMEM((3, TILE_ROWS) + tile, F32),
                pltpu.VMEM((9 * TILE_ROWS, 5) + tile, F32),
                pltpu.VMEM((TILE_ROWS, 5) + tile, F32),
                pltpu.VMEM((9, TILE_ROWS) + tile, F32),
                pltpu.VMEM((group_one, NCOLS), F32),
                pltpu.VMEM((group_two, NCOLS), F32),
            ]
            + [dma((3 + 2 * (pairs // NCOLS),))]
            + [dma((8,)), dma((9,))] * 3
            + [dma((2,))] * 2,
            compiler_params=pltpu.CompilerParams(
                collective_id=0, has_side_effects=True, vmem_limit_bytes=VMEM_BYTES
            ),
        )(
            coords.reshape(4, slots, pairs),
            targets.reshape(2, slots, pairs),
            pair_first.reshape(1, pairs),
            pair_second.reshape(1, pairs),
            pair_count.reshape(1, pairs),
        )
        first_scale, scale_w, scale_g = (scale[None] for scale in scales)
        results = (first_scale * gradient, scale_w * product + scale_g * gradient)
        return tuple(x.reshape(6, SEC_DEV, ROWS_DEV, NCOLS) for x in results)

    return jax.shard_map(
        on_device,
        mesh=mesh,
        in_specs=(
            P(None, None, "sec", "band", None),
            P(None, None, "sec", "band", None),
            P("sec", "band", None),
            P("sec", "band", None),
            P("sec", "band", None),
        ),
        out_specs=(P(None, "sec", "band", None), P(None, "sec", "band", None)),
        check_vma=False,
    )
```

```python
import functools
import math

import jax
import jax.numpy as jnp
from jax import lax
from jax.experimental import pallas as pl
from jax.experimental.pallas import tpu as pltpu
from jax.sharding import PartitionSpec as P

NCOLS = 128
SEC_DEV = 2
ROWS_DEV = 2
TILE_ROWS = SEC_DEV * ROWS_DEV
ROWS_WIDE = ROWS_DEV + 4
MESH = pl.DeviceIdType.MESH
CHUNKS = 5
VMEM_BYTES = 56426496
F32 = jnp.float32
SHIFTS = (-2, -1, 0, 1, 2)
EDGES = (1, 3, 5, 7)
CORNERS = (0, 2, 6, 8)
NEIGHBOURS = ((-1, 0), (1, 0), (0, -1), (0, 1), (-1, -1), (1, -1), (-1, 1), (1, 1))

SUMS = (
    "xp",
    "yp",
    "xq",
    "yq",
    "xpxp",
    "xpyp",
    "ypyp",
    "xqxq",
    "xqyq",
    "yqyq",
    "xpxq",
    "xpyq",
    "ypxq",
    "ypyq",
    "rx",
    "ry",
    "rxxp",
    "rxyp",
    "ryxp",
    "ryyp",
    "rxxq",
    "rxyq",
    "ryxq",
    "ryyq",
)
GROUPS = (
    ("-rxxq", "-rxyq", "-rx", "-ryxq", "-ryyq", "-ry", "0", "0"),
    ("xpxq", "xpyq", "xp", "ypxq", "ypyq", "yp", "code", "0"),
    ("xq", "yq", "n", "xqxq", "xqyq", "yqyq", "0", "0"),
    ("rxxp", "rxyp", "rx", "ryxp", "ryyp", "ry", "0", "0"),
    ("xp", "yp", "n", "xpxp", "xpyp", "ypyp", "0", "0"),
    ("xpxq", "ypxq", "xq", "xpyq", "ypyq", "yq", "0", "0"),
)
TABLE = tuple(name for group in GROUPS for name in group)


def halves(block):
    upper = lax.broadcasted_iota(jnp.int32, (8, NCOLS), 0) < 3
    return jnp.where(upper, block, pltpu.roll(block, 3, 0)), jnp.where(upper, pltpu.roll(block, 5, 0), block)


def row_of(block, upper_row, lower_row):
    upper = lax.broadcasted_iota(jnp.int32, (8, NCOLS), 0) < 3
    one = jnp.broadcast_to(block[upper_row : upper_row + 1], (8, NCOLS))
    two = jnp.broadcast_to(block[lower_row : lower_row + 1], (8, NCOLS))
    return jnp.where(upper, one, two)


def pair_tables(coords_ref, targets_ref, first_ref, second_ref, count_ref, table, ready):
    slots = coords_ref.shape[1]
    pairs = coords_ref.shape[2]
    first = first_ref[...]
    second = second_ref[...]

    def place(index):
        row = lax.shift_right_logical(index, 7)
        section = lax.shift_right_logical(row * 43, 8)
        return section, row - section * ROWS_WIDE, lax.bitwise_and(index, NCOLS - 1)

    near, far = place(first), place(second)
    code = ((far[0] - near[0]) * 16 + far[1] - near[1]) * 16 + far[2] - near[2]
    lines = {"code": code.astype(F32), "n": count_ref[...].astype(F32)}
    squares = jnp.zeros((8, NCOLS), F32)
    for block in range(pairs // NCOLS):
        lanes = pl.ds(block * NCOLS, NCOLS)
        count = jnp.broadcast_to(count_ref[:, lanes], (16, NCOLS))
        ready(block)

        def chunk(k, sums):
            rows = pl.ds(pl.multiple_of(k * 16, 16), 16)
            present = lax.broadcasted_iota(jnp.int32, (16, NCOLS), 0) + k * 16 < count

            def load(ref, i):
                return jnp.where(present, ref[i, rows, lanes].astype(F32), 0.0)

            v = {"xp": load(coords_ref, 0), "yp": load(coords_ref, 1), "xq": load(coords_ref, 2)}
            v.update(yq=load(coords_ref, 3), rx=load(targets_ref, 0), ry=load(targets_ref, 1))
            out = []
            for name, total in zip(SUMS, sums):
                term = v[name] if len(name) == 2 else v[name[:2]] * v[name[2:]]
                out.append(total + (term[:8] + term[8:]))
            square = v["rx"] * v["rx"] + v["ry"] * v["ry"]
            out.append(sums[-1] + (square[:8] + square[8:]))
            return tuple(out)

        def chunks(k, sums):
            for i in range(CHUNKS):
                sums = chunk(k * CHUNKS + i, sums)
            return sums

        zero = jnp.zeros((8, NCOLS), F32)
        sums = (zero,) * len(SUMS) + (squares,)
        sums = lax.fori_loop(0, slots // (16 * CHUNKS), chunks, sums)
        squares = sums[-1]
        totals = {name: jnp.sum(s, axis=0, keepdims=True) for name, s in zip(SUMS, sums)}
        for row, name in enumerate(TABLE):
            if name == "0":
                line = jnp.zeros((1, NCOLS), F32)
            elif name in lines:
                line = lines[name][:, block * NCOLS : (block + 1) * NCOLS]
            elif name[0] == "-":
                line = -totals[name[1:]]
            else:
                line = totals[name]
            table[row : row + 1, lanes] = line
    return squares


def place_table(first_ref, chosen):
    pairs = first_ref.shape[1]
    first = jnp.broadcast_to(first_ref[...], (NCOLS, pairs))
    column = lax.broadcasted_iota(jnp.int32, (NCOLS, pairs), 0)
    for row in range(TILE_ROWS):
        start = ((row // ROWS_DEV + 2) * ROWS_WIDE + row % ROWS_DEV + 2) * NCOLS
        chosen[row] = jnp.where(first == column + start, 1.0, 0.0).astype(jnp.bfloat16)


def by_first_tile(chosen, table, store):
    values = table[...]
    high = values.astype(jnp.bfloat16)
    rest = values - high.astype(F32)
    middle = rest.astype(jnp.bfloat16)
    low = (rest - middle.astype(F32)).astype(jnp.bfloat16)
    parts = jnp.concatenate([high, middle, low], axis=0)
    height = values.shape[0]
    for row in range(TILE_ROWS):
        moved = lax.dot_general(
            parts, chosen[row], (((1,), (1,)), ((), ())), preferred_element_type=F32
        )
        moved = moved[:height] + moved[height : 2 * height] + moved[2 * height :]
        for group in range(len(GROUPS)):
            store(group, row, moved[8 * group : 8 * group + 8])


def row_key(block, row):
    section, band = block // 3 - 1, block % 3 - 1
    return (section * SEC_DEV + row // ROWS_DEV) * 256 + (band * ROWS_DEV + row % ROWS_DEV) * 16


def dynamic_key(block, row):
    section, band = block // 3 - 1, lax.rem(block, 3) - 1
    key = (section * SEC_DEV + row // ROWS_DEV) * 256 + (band * ROWS_DEV + row % ROWS_DEV) * 16
    return key.astype(F32)


def reach(block, row, target_block, target_row):
    section = (target_block // 3 - block // 3) * SEC_DEV + target_row // 2 - row // 2
    across = (target_block % 3 - block % 3) * ROWS_DEV + target_row % 2 - row % 2
    return abs(section) <= 2 and abs(across) <= 2


def turn(value, shift):
    return pltpu.roll(value, shift % NCOLS, 1) if shift else value


def own_keys(terms, moments, keys, moved):
    for row in range(TILE_ROWS):
        code = jnp.broadcast_to(moments[4, 0, row, 6:7, :], (8, NCOLS)) + float(row_key(4, row))
        for i, shift in enumerate(SHIFTS):
            keys[16 + row, i] = turn(code, shift) - float(shift)
            moved[row, i] = turn(terms[row], shift)


def scatter_to(block, keys, moved, out):
    for target in range(TILE_ROWS):
        total = jnp.zeros((8, NCOLS), F32)
        here = float(row_key(block, target))
        for row in range(TILE_ROWS):
            if reach(4, row, block, target):
                for i in range(5):
                    total = total + jnp.where(keys[16 + row, i] == here, moved[row, i], 0.0)
        out(target, total)


def gather_blocks(moments, keys):
    def step(block, totals):
        totals = list(totals)
        for row in range(TILE_ROWS):
            value = moments[block, 1, row]
            code = jnp.broadcast_to(moments[block, 0, row, 6:7, :], (8, NCOLS))
            code = code + dynamic_key(block, row)
            for i, shift in enumerate(SHIFTS):
                key = turn(code, shift) - float(shift)
                keys[block * TILE_ROWS + row, i] = key
                part = turn(value, shift)
                for t in range(TILE_ROWS):
                    hit = key == float(row_key(4, t))
                    totals[t] = totals[t] + jnp.where(hit, part, 0.0)
        return tuple(totals)

    return lax.fori_loop(0, 9, step, (jnp.zeros((8, NCOLS), F32),) * TILE_ROWS)


def own_blocks(block, g):
    upper, lower = halves(block)
    line = lax.rem(lax.broadcasted_iota(jnp.int32, (8, NCOLS), 0), 3)
    xx, xy, yy = (row_of(lower, k, k) for k in range(3))
    x, y = (row_of(upper, k, k) for k in range(2))
    first = jnp.where(line == 0, xx, jnp.where(line == 1, xy, jnp.where(line == 2, x, 0.0)))
    second = jnp.where(line == 0, xy, jnp.where(line == 1, yy, jnp.where(line == 2, y, 0.0)))
    return first * row_of(g, 0, 3) + second * row_of(g, 1, 4) + upper * row_of(g, 2, 5)


def apply_pairs(field, moments, local, keys, landed):
    def step(block, carry):
        far, totals = list(carry[:20]), list(carry[20:])
        for row in range(TILE_ROWS):
            g = field[block, row]
            here = dynamic_key(block, row)
            for t in range(TILE_ROWS):
                for i in range(5):
                    far[t * 5 + i] = jnp.where(keys[16 + t, i] == here, g, far[t * 5 + i])
            by_a, by_b = halves(moments[block, 0, row])
            by_c, _ = halves(moments[block, 1, row])
            value = by_a * row_of(g, 0, 3) + by_b * row_of(g, 1, 4) + by_c * row_of(g, 2, 5)
            for i, shift in enumerate(SHIFTS):
                part = turn(value, shift)
                key = keys[block * TILE_ROWS + row, i]
                for t in range(TILE_ROWS):
                    hit = key == float(row_key(4, t))
                    totals[t] = totals[t] + jnp.where(hit, part, 0.0)
        return tuple(far) + tuple(totals)

    def edge(k, carry):
        landed(2 * k + 1)
        return step(2 * k + 1, carry)

    def corner(k, carry):
        block = 2 * k + 2 * (k // 2)
        landed(block)
        return step(block, carry)

    carry = step(jnp.int32(4), (jnp.zeros((8, NCOLS), F32),) * 24)
    carry = lax.fori_loop(0, len(EDGES), edge, carry)
    carry = lax.fori_loop(0, len(CORNERS), corner, carry)
    out = []
    for t in range(TILE_ROWS):
        far = carry[t * 5 + 2]
        for i, shift in enumerate(SHIFTS):
            if shift:
                far = far + turn(carry[t * 5 + i], -shift)
        by_a, by_b = halves(local[2, t])
        by_c, _ = halves(local[1, t])
        near = by_a * row_of(far, 0, 3) + by_b * row_of(far, 1, 4) + by_c * row_of(far, 2, 5)
        out.append(near + carry[20 + t])
    return out


def kernel(
    sections,
    bands,
    group_one,
    coords_ref,
    targets_ref,
    first_ref,
    second_ref,
    count_ref,
    gradient_ref,
    product_ref,
    solution_scale_ref,
    product_scale_ref,
    gradient_scale_ref,
    coords,
    targets,
    first,
    second,
    count,
    chosen,
    table,
    terms,
    folded,
    arrived,
    moments,
    local,
    keys,
    moved,
    field,
    sums_one,
    sums_two,
    load_sems,
    terms_send,
    terms_recv,
    moments_send,
    moments_recv,
    field_send,
    field_recv,
    sums_send,
    sums_recv,
    met,
):
    sec = lax.axis_index("sec")
    band = lax.axis_index("band")
    place = lax.rem(sec, group_one)
    base = sec - place
    group = lax.div(sec, group_one)

    def neighbour(a, b):
        return (lax.rem(sec + a + sections, sections), lax.rem(band + b + bands, bands))

    groups = sections // group_one

    def far_first(k, count):
        return count // 2 + (2 * lax.rem(k, 2) - 1) * lax.div(k + 1, 2)

    def each_peer_one(act):
        def step(k, carry):
            act((base + lax.rem(place + far_first(k, group_one), group_one), band))
            return carry

        lax.fori_loop(0, group_one - 1, step, 0)

    def each_peer_two(act):
        def step(k, carry):
            other = lax.rem(group + far_first(k, groups), groups) * group_one + place
            for x in range(bands):
                act((other, x))
            return carry

        lax.fori_loop(0, groups - 1, step, 0)
        for x in range(1, bands):
            act((sec, lax.rem(band + x, bands)))

    def half(count):
        return (count // 2 + 1) // 2

    def each_relay(act):
        for d in range(1, half(group_one) + 1):
            for step in (d, group_one - d):
                act((base + lax.rem(place + step, group_one), band))
        for d in range(-half(groups), half(groups) + 1):
            other = lax.rem(group + d + groups, groups) * group_one + place
            for x in range(-half(bands), half(bands) + 1):
                if (d, x) != (0, 0):
                    act((other, lax.rem(band + x + bands, bands)))

    relays = 2 * half(group_one) + (2 * half(groups) + 1) * (2 * half(bands) + 1) - 1

    def signal(semaphore, device):
        pl.semaphore_signal(semaphore, inc=1, device_id=device, device_id_type=MESH)

    barrier = pltpu.get_barrier_semaphore()
    each_relay(functools.partial(signal, barrier))
    for a, b in NEIGHBOURS:
        signal(barrier, neighbour(a, b))

    loads = []

    def load(source, target):
        loads.append(pltpu.make_async_copy(source, target, load_sems.at[len(loads)]))
        loads[-1].start()

    load(count_ref, count)
    load(first_ref, first)
    load(second_ref, second)
    blocks = coords_ref.shape[2] // NCOLS
    for i in range(blocks):
        lanes = pl.ds(i * NCOLS, NCOLS)
        load(coords_ref.at[:, :, lanes], coords.at[:, :, lanes])
        load(targets_ref.at[:, :, lanes], targets.at[:, :, lanes])
    for copy in loads[:3]:
        copy.wait()
    place_table(first, chosen)

    def ready(i):
        loads[3 + 2 * i].wait()
        loads[4 + 2 * i].wait()

    squares = pair_tables(coords, targets, first, second, count, table, ready)

    def store(group, tile_row, value):
        if group == 0:
            terms[tile_row] = value
        elif group < 3:
            moments[4, group - 1, tile_row] = value
        else:
            local[group - 3, tile_row] = value

    by_first_tile(chosen, table, store)
    own_keys(terms, moments, keys, moved)

    pl.semaphore_wait(barrier, 8 + relays)

    def send(source, target, send_sem, recv_sem, i, part=lambda ref: ref.at[:, 0:6]):
        a, b = NEIGHBOURS[i]
        copy = pltpu.make_async_remote_copy(
            src_ref=source,
            dst_ref=part(target.at[(1 - a) * 3 + 1 - b]),
            send_sem=send_sem.at[i],
            recv_sem=recv_sem.at[(1 - a) * 3 + 1 - b],
            device_id=neighbour(a, b),
            device_id_type=MESH,
        )
        copy.start()
        return copy

    def landed(ref, sem):
        pltpu.make_async_copy(ref, ref, sem).wait()

    terms_copies = []
    for i, (a, b) in enumerate(NEIGHBOURS):
        block = (a + 1) * 3 + b + 1

        def put(t, value, block=block):
            folded[block, t] = value

        scatter_to(block, keys, moved, put)
        terms_copies.append(send(folded.at[block, :, 0:6], arrived, terms_send, terms_recv, i))
    moments_copies = []
    for i in range(8):
        moments_copies.append(send(moments.at[4], moments, moments_send, moments_recv, i, lambda ref: ref))

    each_relay(functools.partial(signal, met))

    gradient = [None] * TILE_ROWS

    def keep(t, value):
        gradient[t] = value + local[0, t]

    scatter_to(4, keys, moved, keep)
    for block in EDGES + CORNERS:
        landed(arrived.at[block, :, 0:6], terms_recv.at[block])
        for t in range(TILE_ROWS):
            gradient[t] = gradient[t] + arrived[block, t]
    held = lax.broadcasted_iota(jnp.int32, (8, NCOLS), 0) < 6
    for t in range(TILE_ROWS):
        gradient[t] = jnp.where(held, gradient[t], 0.0)
        field[4, t] = gradient[t]
    field_copies = []
    for i in range(8):
        field_copies.append(send(field.at[4, :, 0:6], field, field_send, field_recv, i))

    for block in EDGES + CORNERS:
        landed(moments.at[block], moments_recv.at[block])
    zero = jnp.zeros((8, NCOLS), F32)
    gg = zero
    own = []
    for t, block in enumerate(gather_blocks(moments, keys)):
        gg = gg + gradient[t] * gradient[t]
        own.append(own_blocks(block + local[1, t], gradient[t]))

    def field_landed(block):
        landed(field.at[block, :, 0:6], field_recv.at[block])

    others = apply_pairs(field, moments, local, keys, field_landed)
    wg, ww = zero, zero
    product = []
    for t in range(TILE_ROWS):
        w = jnp.where(held, own[t] - others[t], 0.0)
        product.append(w)
        wg = wg + w * gradient[t]
        ww = ww + w * w

    for t in range(TILE_ROWS):
        for k in range(6):
            gradient_ref[k, t : t + 1, :] = gradient[t][k : k + 1]
            product_ref[k, t : t + 1, :] = product[t][k : k + 1]

    lane = lax.broadcasted_iota(jnp.int32, (1, NCOLS), 1)
    line = jnp.zeros((1, NCOLS), F32)
    for k, part in enumerate((squares, gg, wg, ww)):
        total = jnp.sum(jnp.sum(part, axis=0, keepdims=True), axis=1, keepdims=True)
        line = jnp.where(lane == k, total, line)

    def spread_sum(line, buffer, each_peer, mine, i):
        own = buffer.at[pl.ds(mine, 1), :]
        buffer[pl.ds(mine, 1), :] = line

        def send_to(device):
            pltpu.make_async_remote_copy(
                src_ref=own,
                dst_ref=own,
                send_sem=sums_send.at[i],
                recv_sem=sums_recv.at[i],
                device_id=device,
                device_id_type=MESH,
            ).start()

        each_peer(send_to)
        others = buffer.at[pl.ds(1, buffer.shape[0] - 1), :]
        pltpu.make_async_copy(others, others, sums_recv.at[i]).wait()
        return jnp.sum(buffer[...], axis=0, keepdims=True)

    pl.semaphore_wait(met, relays)
    line = spread_sum(line, sums_one, each_peer_one, place, 0)
    line = spread_sum(line, sums_two, each_peer_two, group * bands + band, 1)

    rr, gg, wg, ww = (jnp.broadcast_to(line[:, k : k + 1], (1, NCOLS)) for k in range(4))
    beta_one = jnp.sqrt(rr)
    norm_g = jnp.sqrt(gg)
    alpha_one = norm_g / beta_one
    beta_two_sq = wg / gg - alpha_one * alpha_one
    beta_two = jnp.sqrt(beta_two_sq)
    on_w = 1.0 / (norm_g * beta_two)
    on_g = -(alpha_one / (beta_one * beta_two) + beta_two / norm_g)
    scaled = on_g / on_w
    alpha_two = on_w * jnp.sqrt(ww + scaled * (2.0 * wg + scaled * gg))
    rho_sq = alpha_one * alpha_one + beta_two_sq
    first_scale = alpha_one * beta_one / (rho_sq * norm_g)
    root = math.sqrt(float(6 * TILE_ROWS * NCOLS * sections * bands))
    scale_w = root * on_w / alpha_two
    scale_g = root * (on_g / alpha_two - beta_two * alpha_two / (rho_sq * norm_g))
    solution_scale_ref[...] = first_scale
    product_scale_ref[...] = scale_w
    gradient_scale_ref[...] = scale_g

    for copies in (terms_copies, moments_copies, field_copies):
        for copy in copies:
            copy.wait_send()
    for i, buffer in enumerate((sums_one, sums_two)):
        others = buffer.at[pl.ds(1, buffer.shape[0] - 1), :]
        pltpu.make_async_copy(others, others, sums_send.at[i]).wait()


def solution(mesh):
    sections, bands = mesh.shape["sec"], mesh.shape["band"]
    group_one = 24 if sections % 24 == 0 else 2
    group_two = sections // group_one * bands

    def on_device(targets, coords, pair_first, pair_second, pair_count):
        slots, pairs = coords.shape[1], coords.shape[-1]
        vmem = pl.BlockSpec(memory_space=pltpu.VMEM)
        anywhere = pl.BlockSpec(memory_space=pl.ANY)
        shape = (6, TILE_ROWS, NCOLS)
        tile = (8, NCOLS)
        dma = pltpu.SemaphoreType.DMA
        gradient, product, *scales = pl.pallas_call(
            functools.partial(kernel, sections, bands, group_one),
            out_shape=tuple(jax.ShapeDtypeStruct(s, F32) for s in (shape, shape) + ((1, NCOLS),) * 3),
            in_specs=[anywhere] * 5,
            out_specs=(vmem,) * 5,
            scratch_shapes=[
                pltpu.VMEM((4, slots, pairs), coords.dtype),
                pltpu.VMEM((2, slots, pairs), targets.dtype),
                pltpu.VMEM((1, pairs), jnp.int32),
                pltpu.VMEM((1, pairs), jnp.int32),
                pltpu.VMEM((1, pairs), jnp.int32),
                pltpu.VMEM((TILE_ROWS, NCOLS, pairs), jnp.bfloat16),
                pltpu.VMEM((8 * len(GROUPS), pairs), F32),
                pltpu.VMEM((TILE_ROWS,) + tile, F32),
                pltpu.VMEM((9, TILE_ROWS) + tile, F32),
                pltpu.VMEM((9, TILE_ROWS) + tile, F32),
                pltpu.VMEM((9, 2, TILE_ROWS) + tile, F32),
                pltpu.VMEM((3, TILE_ROWS) + tile, F32),
                pltpu.VMEM((9 * TILE_ROWS, 5) + tile, F32),
                pltpu.VMEM((TILE_ROWS, 5) + tile, F32),
                pltpu.VMEM((9, TILE_ROWS) + tile, F32),
                pltpu.VMEM((group_one, NCOLS), F32),
                pltpu.VMEM((group_two, NCOLS), F32),
            ]
            + [dma((3 + 2 * (pairs // NCOLS),))]
            + [dma((8,)), dma((9,))] * 3
            + [dma((2,))] * 2
            + [pltpu.SemaphoreType.REGULAR],
            compiler_params=pltpu.CompilerParams(
                collective_id=0, has_side_effects=True, vmem_limit_bytes=VMEM_BYTES
            ),
        )(
            coords.reshape(4, slots, pairs),
            targets.reshape(2, slots, pairs),
            pair_first.reshape(1, pairs),
            pair_second.reshape(1, pairs),
            pair_count.reshape(1, pairs),
        )
        first_scale, scale_w, scale_g = (scale[None] for scale in scales)
        results = (first_scale * gradient, scale_w * product + scale_g * gradient)
        return tuple(x.reshape(6, SEC_DEV, ROWS_DEV, NCOLS) for x in results)

    return jax.shard_map(
        on_device,
        mesh=mesh,
        in_specs=(
            P(None, None, "sec", "band", None),
            P(None, None, "sec", "band", None),
            P("sec", "band", None),
            P("sec", "band", None),
            P("sec", "band", None),
        ),
        out_specs=(P(None, "sec", "band", None), P(None, "sec", "band", None)),
        check_vma=False,
    )
```

```python
import functools
import math

import jax
import jax.numpy as jnp
from jax import lax
from jax.experimental import pallas as pl
from jax.experimental.pallas import tpu as pltpu
from jax.sharding import PartitionSpec as P

NCOLS = 128
SEC_DEV = 2
ROWS_DEV = 2
TILE_ROWS = SEC_DEV * ROWS_DEV
ROWS_WIDE = ROWS_DEV + 4
MESH = pl.DeviceIdType.MESH
CHUNKS = 5
VMEM_BYTES = 56426496
F32 = jnp.float32
SHIFTS = (-2, -1, 0, 1, 2)
EDGES = (1, 3, 5, 7)
CORNERS = (0, 2, 6, 8)
NEIGHBOURS = ((-1, 0), (1, 0), (0, -1), (0, 1), (-1, -1), (1, -1), (-1, 1), (1, 1))

SUMS = (
    "xp",
    "yp",
    "xq",
    "yq",
    "xpxp",
    "xpyp",
    "ypyp",
    "xqxq",
    "xqyq",
    "yqyq",
    "xpxq",
    "xpyq",
    "ypxq",
    "ypyq",
    "rx",
    "ry",
    "rxxp",
    "rxyp",
    "ryxp",
    "ryyp",
    "rxxq",
    "rxyq",
    "ryxq",
    "ryyq",
)
GROUPS = (
    ("-rxxq", "-rxyq", "-rx", "-ryxq", "-ryyq", "-ry", "0", "0"),
    ("xpxq", "xpyq", "xp", "ypxq", "ypyq", "yp", "code", "0"),
    ("xq", "yq", "n", "xqxq", "xqyq", "yqyq", "0", "0"),
    ("rxxp", "rxyp", "rx", "ryxp", "ryyp", "ry", "0", "0"),
    ("xp", "yp", "n", "xpxp", "xpyp", "ypyp", "0", "0"),
    ("xpxq", "ypxq", "xq", "xpyq", "ypyq", "yq", "0", "0"),
)
TABLE = tuple(name for group in GROUPS for name in group)


def halves(block):
    upper = lax.broadcasted_iota(jnp.int32, (8, NCOLS), 0) < 3
    return jnp.where(upper, block, pltpu.roll(block, 3, 0)), jnp.where(upper, pltpu.roll(block, 5, 0), block)


def row_of(block, upper_row, lower_row):
    upper = lax.broadcasted_iota(jnp.int32, (8, NCOLS), 0) < 3
    one = jnp.broadcast_to(block[upper_row : upper_row + 1], (8, NCOLS))
    two = jnp.broadcast_to(block[lower_row : lower_row + 1], (8, NCOLS))
    return jnp.where(upper, one, two)


def pair_tables(coords_ref, targets_ref, first_ref, second_ref, count_ref, table, ready):
    slots = coords_ref.shape[1]
    pairs = coords_ref.shape[2]
    first = first_ref[...]
    second = second_ref[...]

    def place(index):
        row = lax.shift_right_logical(index, 7)
        section = lax.shift_right_logical(row * 43, 8)
        return section, row - section * ROWS_WIDE, lax.bitwise_and(index, NCOLS - 1)

    near, far = place(first), place(second)
    code = ((far[0] - near[0]) * 16 + far[1] - near[1]) * 16 + far[2] - near[2]
    lines = {"code": code.astype(F32), "n": count_ref[...].astype(F32)}
    squares = jnp.zeros((8, NCOLS), F32)
    for block in range(pairs // NCOLS):
        lanes = pl.ds(block * NCOLS, NCOLS)
        count = jnp.broadcast_to(count_ref[:, lanes], (16, NCOLS))
        ready(block)

        def chunk(k, sums):
            rows = pl.ds(pl.multiple_of(k * 16, 16), 16)
            present = lax.broadcasted_iota(jnp.int32, (16, NCOLS), 0) + k * 16 < count

            def load(ref, i):
                return jnp.where(present, ref[i, rows, lanes].astype(F32), 0.0)

            v = {"xp": load(coords_ref, 0), "yp": load(coords_ref, 1), "xq": load(coords_ref, 2)}
            v.update(yq=load(coords_ref, 3), rx=load(targets_ref, 0), ry=load(targets_ref, 1))
            out = []
            for name, total in zip(SUMS, sums):
                term = v[name] if len(name) == 2 else v[name[:2]] * v[name[2:]]
                out.append(total + (term[:8] + term[8:]))
            square = v["rx"] * v["rx"] + v["ry"] * v["ry"]
            out.append(sums[-1] + (square[:8] + square[8:]))
            return tuple(out)

        def chunks(k, sums):
            for i in range(CHUNKS):
                sums = chunk(k * CHUNKS + i, sums)
            return sums

        zero = jnp.zeros((8, NCOLS), F32)
        sums = (zero,) * len(SUMS) + (squares,)
        sums = lax.fori_loop(0, slots // (16 * CHUNKS), chunks, sums)
        squares = sums[-1]
        totals = {name: jnp.sum(s, axis=0, keepdims=True) for name, s in zip(SUMS, sums)}
        for row, name in enumerate(TABLE):
            if name == "0":
                line = jnp.zeros((1, NCOLS), F32)
            elif name in lines:
                line = lines[name][:, block * NCOLS : (block + 1) * NCOLS]
            elif name[0] == "-":
                line = -totals[name[1:]]
            else:
                line = totals[name]
            table[row : row + 1, lanes] = line
    return squares


def place_table(first_ref, chosen):
    pairs = first_ref.shape[1]
    first = jnp.broadcast_to(first_ref[...], (NCOLS, pairs))
    column = lax.broadcasted_iota(jnp.int32, (NCOLS, pairs), 0)
    for row in range(TILE_ROWS):
        start = ((row // ROWS_DEV + 2) * ROWS_WIDE + row % ROWS_DEV + 2) * NCOLS
        chosen[row] = jnp.where(first == column + start, 1.0, 0.0).astype(jnp.bfloat16)


def by_first_tile(chosen, table, store):
    values = table[...]
    high = values.astype(jnp.bfloat16)
    rest = values - high.astype(F32)
    middle = rest.astype(jnp.bfloat16)
    low = (rest - middle.astype(F32)).astype(jnp.bfloat16)
    parts = jnp.concatenate([high, middle, low], axis=0)
    height = values.shape[0]
    for row in range(TILE_ROWS):
        moved = lax.dot_general(
            parts, chosen[row], (((1,), (1,)), ((), ())), preferred_element_type=F32
        )
        moved = moved[:height] + moved[height : 2 * height] + moved[2 * height :]
        for group in range(len(GROUPS)):
            store(group, row, moved[8 * group : 8 * group + 8])


def row_key(block, row):
    section, band = block // 3 - 1, block % 3 - 1
    return (section * SEC_DEV + row // ROWS_DEV) * 256 + (band * ROWS_DEV + row % ROWS_DEV) * 16


def dynamic_key(block, row):
    section, band = block // 3 - 1, lax.rem(block, 3) - 1
    key = (section * SEC_DEV + row // ROWS_DEV) * 256 + (band * ROWS_DEV + row % ROWS_DEV) * 16
    return key.astype(F32)


def reach(block, row, target_block, target_row):
    section = (target_block // 3 - block // 3) * SEC_DEV + target_row // 2 - row // 2
    across = (target_block % 3 - block % 3) * ROWS_DEV + target_row % 2 - row % 2
    return abs(section) <= 2 and abs(across) <= 2


def turn(value, shift):
    return pltpu.roll(value, shift % NCOLS, 1) if shift else value


def own_keys(terms, moments, keys, moved):
    for row in range(TILE_ROWS):
        code = jnp.broadcast_to(moments[4, 0, row, 6:7, :], (8, NCOLS)) + float(row_key(4, row))
        for i, shift in enumerate(SHIFTS):
            keys[16 + row, i] = turn(code, shift) - float(shift)
            moved[row, i] = turn(terms[row], shift)


def scatter_to(block, keys, moved, out):
    for target in range(TILE_ROWS):
        total = jnp.zeros((8, NCOLS), F32)
        here = float(row_key(block, target))
        for row in range(TILE_ROWS):
            if reach(4, row, block, target):
                for i in range(5):
                    total = total + jnp.where(keys[16 + row, i] == here, moved[row, i], 0.0)
        out(target, total)


def gather_blocks(moments, keys):
    def step(block, totals):
        totals = list(totals)
        for row in range(TILE_ROWS):
            value = moments[block, 1, row]
            code = jnp.broadcast_to(moments[block, 0, row, 6:7, :], (8, NCOLS))
            code = code + dynamic_key(block, row)
            for i, shift in enumerate(SHIFTS):
                key = turn(code, shift) - float(shift)
                keys[block * TILE_ROWS + row, i] = key
                part = turn(value, shift)
                for t in range(TILE_ROWS):
                    hit = key == float(row_key(4, t))
                    totals[t] = totals[t] + jnp.where(hit, part, 0.0)
        return tuple(totals)

    return lax.fori_loop(0, 9, step, (jnp.zeros((8, NCOLS), F32),) * TILE_ROWS)


def own_blocks(block, g):
    upper, lower = halves(block)
    line = lax.rem(lax.broadcasted_iota(jnp.int32, (8, NCOLS), 0), 3)
    xx, xy, yy = (row_of(lower, k, k) for k in range(3))
    x, y = (row_of(upper, k, k) for k in range(2))
    first = jnp.where(line == 0, xx, jnp.where(line == 1, xy, jnp.where(line == 2, x, 0.0)))
    second = jnp.where(line == 0, xy, jnp.where(line == 1, yy, jnp.where(line == 2, y, 0.0)))
    return first * row_of(g, 0, 3) + second * row_of(g, 1, 4) + upper * row_of(g, 2, 5)


def apply_pairs(field, moments, local, keys, landed):
    def step(block, carry):
        far, totals = list(carry[:20]), list(carry[20:])
        for row in range(TILE_ROWS):
            g = field[block, row]
            here = dynamic_key(block, row)
            for t in range(TILE_ROWS):
                for i in range(5):
                    far[t * 5 + i] = jnp.where(keys[16 + t, i] == here, g, far[t * 5 + i])
            by_a, by_b = halves(moments[block, 0, row])
            by_c, _ = halves(moments[block, 1, row])
            value = by_a * row_of(g, 0, 3) + by_b * row_of(g, 1, 4) + by_c * row_of(g, 2, 5)
            for i, shift in enumerate(SHIFTS):
                part = turn(value, shift)
                key = keys[block * TILE_ROWS + row, i]
                for t in range(TILE_ROWS):
                    hit = key == float(row_key(4, t))
                    totals[t] = totals[t] + jnp.where(hit, part, 0.0)
        return tuple(far) + tuple(totals)

    def edge(k, carry):
        landed(2 * k + 1)
        return step(2 * k + 1, carry)

    def corner(k, carry):
        block = 2 * k + 2 * (k // 2)
        landed(block)
        return step(block, carry)

    carry = step(jnp.int32(4), (jnp.zeros((8, NCOLS), F32),) * 24)
    carry = lax.fori_loop(0, len(EDGES), edge, carry)
    carry = lax.fori_loop(0, len(CORNERS), corner, carry)
    out = []
    for t in range(TILE_ROWS):
        far = carry[t * 5 + 2]
        for i, shift in enumerate(SHIFTS):
            if shift:
                far = far + turn(carry[t * 5 + i], -shift)
        by_a, by_b = halves(local[2, t])
        by_c, _ = halves(local[1, t])
        near = by_a * row_of(far, 0, 3) + by_b * row_of(far, 1, 4) + by_c * row_of(far, 2, 5)
        out.append(near + carry[20 + t])
    return out


def kernel(
    sections,
    bands,
    group_one,
    coords_ref,
    targets_ref,
    first_ref,
    second_ref,
    count_ref,
    gradient_ref,
    product_ref,
    solution_scale_ref,
    product_scale_ref,
    gradient_scale_ref,
    coords,
    targets,
    first,
    second,
    count,
    chosen,
    table,
    terms,
    folded,
    arrived,
    moments,
    local,
    keys,
    moved,
    field,
    sums_one,
    sums_two,
    load_sems,
    terms_send,
    terms_recv,
    moments_send,
    moments_recv,
    field_send,
    field_recv,
    sums_send,
    sums_recv,
    met,
):
    sec = lax.axis_index("sec")
    band = lax.axis_index("band")
    place = lax.rem(sec, group_one)
    base = sec - place
    group = lax.div(sec, group_one)

    def neighbour(a, b):
        return (lax.rem(sec + a + sections, sections), lax.rem(band + b + bands, bands))

    loads = []

    def load(source, target):
        loads.append(pltpu.make_async_copy(source, target, load_sems.at[len(loads)]))
        loads[-1].start()

    load(count_ref, count)
    load(first_ref, first)
    load(second_ref, second)
    blocks = coords_ref.shape[2] // NCOLS
    for i in range(blocks):
        lanes = pl.ds(i * NCOLS, NCOLS)
        load(coords_ref.at[:, :, lanes], coords.at[:, :, lanes])
        load(targets_ref.at[:, :, lanes], targets.at[:, :, lanes])
    groups = sections // group_one

    def far_first(k, count):
        return count // 2 + (2 * lax.rem(k, 2) - 1) * lax.div(k + 1, 2)

    def each_peer_one(act):
        def step(k, carry):
            act((base + lax.rem(place + far_first(k, group_one), group_one), band))
            return carry

        lax.fori_loop(0, group_one - 1, step, 0)

    def each_peer_two(act):
        def step(k, carry):
            other = lax.rem(group + far_first(k, groups), groups) * group_one + place
            for x in range(bands):
                act((other, x))
            return carry

        lax.fori_loop(0, groups - 1, step, 0)
        for x in range(1, bands):
            act((sec, lax.rem(band + x, bands)))

    def half(count):
        return (count // 2 + 1) // 2

    def each_relay(act):
        for d in range(1, half(group_one) + 1):
            for step in (d, group_one - d):
                act((base + lax.rem(place + step, group_one), band))
        for d in range(-half(groups), half(groups) + 1):
            other = lax.rem(group + d + groups, groups) * group_one + place
            for x in range(-half(bands), half(bands) + 1):
                if (d, x) != (0, 0):
                    act((other, lax.rem(band + x + bands, bands)))

    relays = 2 * half(group_one) + (2 * half(groups) + 1) * (2 * half(bands) + 1) - 1

    def signal(semaphore, device):
        pl.semaphore_signal(semaphore, inc=1, device_id=device, device_id_type=MESH)

    barrier = pltpu.get_barrier_semaphore()
    each_relay(functools.partial(signal, barrier))
    for a, b in NEIGHBOURS:
        signal(barrier, neighbour(a, b))

    for copy in loads[:3]:
        copy.wait()
    place_table(first, chosen)

    def ready(i):
        loads[3 + 2 * i].wait()
        loads[4 + 2 * i].wait()

    squares = pair_tables(coords, targets, first, second, count, table, ready)

    def store(group, tile_row, value):
        if group == 0:
            terms[tile_row] = value
        elif group < 3:
            moments[4, group - 1, tile_row] = value
        else:
            local[group - 3, tile_row] = value

    by_first_tile(chosen, table, store)
    own_keys(terms, moments, keys, moved)
    gradient = [None] * TILE_ROWS
    for block in range(9):

        def put(t, value, block=block):
            if block == 4:
                gradient[t] = value + local[0, t]
            else:
                folded[block, t] = value

        scatter_to(block, keys, moved, put)

    pl.semaphore_wait(barrier, 8 + relays)

    def send(source, target, send_sem, recv_sem, i, part=lambda ref: ref.at[:, 0:6]):
        a, b = NEIGHBOURS[i]
        copy = pltpu.make_async_remote_copy(
            src_ref=source,
            dst_ref=part(target.at[(1 - a) * 3 + 1 - b]),
            send_sem=send_sem.at[i],
            recv_sem=recv_sem.at[(1 - a) * 3 + 1 - b],
            device_id=neighbour(a, b),
            device_id_type=MESH,
        )
        copy.start()
        return copy

    def landed(ref, sem):
        pltpu.make_async_copy(ref, ref, sem).wait()

    terms_copies = []
    for i, (a, b) in enumerate(NEIGHBOURS):
        source = folded.at[(a + 1) * 3 + b + 1, :, 0:6]
        terms_copies.append(send(source, arrived, terms_send, terms_recv, i))
    moments_copies = []
    for i in range(8):
        moments_copies.append(send(moments.at[4], moments, moments_send, moments_recv, i, lambda ref: ref))

    each_relay(functools.partial(signal, met))

    for block in EDGES + CORNERS:
        landed(arrived.at[block, :, 0:6], terms_recv.at[block])
        for t in range(TILE_ROWS):
            gradient[t] = gradient[t] + arrived[block, t]
    held = lax.broadcasted_iota(jnp.int32, (8, NCOLS), 0) < 6
    for t in range(TILE_ROWS):
        gradient[t] = jnp.where(held, gradient[t], 0.0)
        field[4, t] = gradient[t]
    field_copies = []
    for i in range(8):
        field_copies.append(send(field.at[4, :, 0:6], field, field_send, field_recv, i))

    for block in EDGES + CORNERS:
        landed(moments.at[block], moments_recv.at[block])
    zero = jnp.zeros((8, NCOLS), F32)
    gg = zero
    own = []
    for t, block in enumerate(gather_blocks(moments, keys)):
        gg = gg + gradient[t] * gradient[t]
        own.append(own_blocks(block + local[1, t], gradient[t]))

    def whole(part):
        return jnp.sum(jnp.sum(part, axis=0, keepdims=True), axis=1, keepdims=True)

    lane = lax.broadcasted_iota(jnp.int32, (1, NCOLS), 1)
    line = jnp.where(lane == 0, whole(squares), jnp.where(lane == 1, whole(gg), 0.0))

    def field_landed(block):
        landed(field.at[block, :, 0:6], field_recv.at[block])

    others = apply_pairs(field, moments, local, keys, field_landed)
    wg, ww = zero, zero
    product = []
    for t in range(TILE_ROWS):
        w = jnp.where(held, own[t] - others[t], 0.0)
        product.append(w)
        wg = wg + w * gradient[t]
        ww = ww + w * w

    for k, part in ((2, wg), (3, ww)):
        line = jnp.where(lane == k, whole(part), line)

    def store_results():
        for t in range(TILE_ROWS):
            for k in range(6):
                gradient_ref[k, t : t + 1, :] = gradient[t][k : k + 1]
                product_ref[k, t : t + 1, :] = product[t][k : k + 1]

    def spread_sum(line, buffer, each_peer, mine, i, meanwhile):
        own = buffer.at[pl.ds(mine, 1), :]
        buffer[pl.ds(mine, 1), :] = line

        def send_to(device):
            pltpu.make_async_remote_copy(
                src_ref=own,
                dst_ref=own,
                send_sem=sums_send.at[i],
                recv_sem=sums_recv.at[i],
                device_id=device,
                device_id_type=MESH,
            ).start()

        each_peer(send_to)
        meanwhile()
        others = buffer.at[pl.ds(1, buffer.shape[0] - 1), :]
        pltpu.make_async_copy(others, others, sums_recv.at[i]).wait()
        return jnp.sum(buffer[...], axis=0, keepdims=True)

    pl.semaphore_wait(met, relays)
    line = spread_sum(line, sums_one, each_peer_one, place, 0, store_results)
    line = spread_sum(line, sums_two, each_peer_two, group * bands + band, 1, lambda: None)

    rr, gg, wg, ww = (jnp.broadcast_to(line[:, k : k + 1], (1, NCOLS)) for k in range(4))
    beta_one = jnp.sqrt(rr)
    norm_g = jnp.sqrt(gg)
    alpha_one = norm_g / beta_one
    beta_two_sq = wg / gg - alpha_one * alpha_one
    beta_two = jnp.sqrt(beta_two_sq)
    on_w = 1.0 / (norm_g * beta_two)
    on_g = -(alpha_one / (beta_one * beta_two) + beta_two / norm_g)
    scaled = on_g / on_w
    alpha_two = on_w * jnp.sqrt(ww + scaled * (2.0 * wg + scaled * gg))
    rho_sq = alpha_one * alpha_one + beta_two_sq
    first_scale = alpha_one * beta_one / (rho_sq * norm_g)
    root = math.sqrt(float(6 * TILE_ROWS * NCOLS * sections * bands))
    scale_w = root * on_w / alpha_two
    scale_g = root * (on_g / alpha_two - beta_two * alpha_two / (rho_sq * norm_g))
    solution_scale_ref[...] = first_scale
    product_scale_ref[...] = scale_w
    gradient_scale_ref[...] = scale_g

    for copies in (terms_copies, moments_copies, field_copies):
        for copy in copies:
            copy.wait_send()
    for i, buffer in enumerate((sums_one, sums_two)):
        others = buffer.at[pl.ds(1, buffer.shape[0] - 1), :]
        pltpu.make_async_copy(others, others, sums_send.at[i]).wait()


def solution(mesh):
    sections, bands = mesh.shape["sec"], mesh.shape["band"]
    group_one = 24 if sections % 24 == 0 else 2
    group_two = sections // group_one * bands

    def on_device(targets, coords, pair_first, pair_second, pair_count):
        slots, pairs = coords.shape[1], coords.shape[-1]
        vmem = pl.BlockSpec(memory_space=pltpu.VMEM)
        anywhere = pl.BlockSpec(memory_space=pl.ANY)
        shape = (6, TILE_ROWS, NCOLS)
        tile = (8, NCOLS)
        dma = pltpu.SemaphoreType.DMA
        gradient, product, *scales = pl.pallas_call(
            functools.partial(kernel, sections, bands, group_one),
            out_shape=tuple(jax.ShapeDtypeStruct(s, F32) for s in (shape, shape) + ((1, NCOLS),) * 3),
            in_specs=[anywhere] * 5,
            out_specs=(vmem,) * 5,
            scratch_shapes=[
                pltpu.VMEM((4, slots, pairs), coords.dtype),
                pltpu.VMEM((2, slots, pairs), targets.dtype),
                pltpu.VMEM((1, pairs), jnp.int32),
                pltpu.VMEM((1, pairs), jnp.int32),
                pltpu.VMEM((1, pairs), jnp.int32),
                pltpu.VMEM((TILE_ROWS, NCOLS, pairs), jnp.bfloat16),
                pltpu.VMEM((8 * len(GROUPS), pairs), F32),
                pltpu.VMEM((TILE_ROWS,) + tile, F32),
                pltpu.VMEM((9, TILE_ROWS) + tile, F32),
                pltpu.VMEM((9, TILE_ROWS) + tile, F32),
                pltpu.VMEM((9, 2, TILE_ROWS) + tile, F32),
                pltpu.VMEM((3, TILE_ROWS) + tile, F32),
                pltpu.VMEM((9 * TILE_ROWS, 5) + tile, F32),
                pltpu.VMEM((TILE_ROWS, 5) + tile, F32),
                pltpu.VMEM((9, TILE_ROWS) + tile, F32),
                pltpu.VMEM((group_one, NCOLS), F32),
                pltpu.VMEM((group_two, NCOLS), F32),
            ]
            + [dma((3 + 2 * (pairs // NCOLS),))]
            + [dma((8,)), dma((9,))] * 3
            + [dma((2,))] * 2
            + [pltpu.SemaphoreType.REGULAR],
            compiler_params=pltpu.CompilerParams(
                collective_id=0, has_side_effects=True, vmem_limit_bytes=VMEM_BYTES
            ),
        )(
            coords.reshape(4, slots, pairs),
            targets.reshape(2, slots, pairs),
            pair_first.reshape(1, pairs),
            pair_second.reshape(1, pairs),
            pair_count.reshape(1, pairs),
        )
        first_scale, scale_w, scale_g = (scale[None] for scale in scales)
        results = (first_scale * gradient, scale_w * product + scale_g * gradient)
        return tuple(x.reshape(6, SEC_DEV, ROWS_DEV, NCOLS) for x in results)

    return jax.shard_map(
        on_device,
        mesh=mesh,
        in_specs=(
            P(None, None, "sec", "band", None),
            P(None, None, "sec", "band", None),
            P("sec", "band", None),
            P("sec", "band", None),
            P("sec", "band", None),
        ),
        out_specs=(P(None, "sec", "band", None), P(None, "sec", "band", None)),
        check_vma=False,
    )
```

```python
import functools
import math

import jax
import jax.numpy as jnp
from jax import lax
from jax.experimental import pallas as pl
from jax.experimental.pallas import tpu as pltpu
from jax.sharding import PartitionSpec as P

NCOLS = 128
SEC_DEV = 2
ROWS_DEV = 2
TILE_ROWS = SEC_DEV * ROWS_DEV
ROWS_WIDE = ROWS_DEV + 4
MESH = pl.DeviceIdType.MESH
CHUNKS = 5
VMEM_BYTES = 56426496
F32 = jnp.float32
SHIFTS = (-2, -1, 0, 1, 2)
EDGES = (1, 3, 5, 7)
CORNERS = (0, 2, 6, 8)
NEIGHBOURS = ((-1, 0), (1, 0), (0, -1), (0, 1), (-1, -1), (1, -1), (-1, 1), (1, 1))

SUMS = (
    "xp",
    "yp",
    "xq",
    "yq",
    "xpxp",
    "xpyp",
    "ypyp",
    "xqxq",
    "xqyq",
    "yqyq",
    "xpxq",
    "xpyq",
    "ypxq",
    "ypyq",
    "rx",
    "ry",
    "rxxp",
    "rxyp",
    "ryxp",
    "ryyp",
    "rxxq",
    "rxyq",
    "ryxq",
    "ryyq",
)
GROUPS = (
    ("-rxxq", "-rxyq", "-rx", "-ryxq", "-ryyq", "-ry", "0", "0"),
    ("xpxq", "xpyq", "xp", "ypxq", "ypyq", "yp", "code", "0"),
    ("xq", "yq", "n", "xqxq", "xqyq", "yqyq", "0", "0"),
    ("rxxp", "rxyp", "rx", "ryxp", "ryyp", "ry", "0", "0"),
    ("xp", "yp", "n", "xpxp", "xpyp", "ypyp", "0", "0"),
    ("xpxq", "ypxq", "xq", "xpyq", "ypyq", "yq", "0", "0"),
)
TABLE = tuple(name for group in GROUPS for name in group)


def halves(block):
    upper = lax.broadcasted_iota(jnp.int32, (8, NCOLS), 0) < 3
    return jnp.where(upper, block, pltpu.roll(block, 3, 0)), jnp.where(upper, pltpu.roll(block, 5, 0), block)


def row_of(block, upper_row, lower_row):
    upper = lax.broadcasted_iota(jnp.int32, (8, NCOLS), 0) < 3
    one = jnp.broadcast_to(block[upper_row : upper_row + 1], (8, NCOLS))
    two = jnp.broadcast_to(block[lower_row : lower_row + 1], (8, NCOLS))
    return jnp.where(upper, one, two)


def pair_tables(coords_ref, targets_ref, first_ref, second_ref, count_ref, table, ready):
    slots = coords_ref.shape[1]
    pairs = coords_ref.shape[2]
    first = first_ref[...]
    second = second_ref[...]

    def place(index):
        row = lax.shift_right_logical(index, 7)
        section = lax.shift_right_logical(row * 43, 8)
        return section, row - section * ROWS_WIDE, lax.bitwise_and(index, NCOLS - 1)

    near, far = place(first), place(second)
    code = ((far[0] - near[0]) * 16 + far[1] - near[1]) * 16 + far[2] - near[2]
    lines = {"code": code.astype(F32), "n": count_ref[...].astype(F32)}
    squares = jnp.zeros((8, NCOLS), F32)
    for block in range(pairs // NCOLS):
        lanes = pl.ds(block * NCOLS, NCOLS)
        count = jnp.broadcast_to(count_ref[:, lanes], (16, NCOLS))
        ready(block)

        def chunk(k, sums):
            rows = pl.ds(pl.multiple_of(k * 16, 16), 16)
            present = lax.broadcasted_iota(jnp.int32, (16, NCOLS), 0) + k * 16 < count

            def load(ref, i):
                return jnp.where(present, ref[i, rows, lanes].astype(F32), 0.0)

            v = {"xp": load(coords_ref, 0), "yp": load(coords_ref, 1), "xq": load(coords_ref, 2)}
            v.update(yq=load(coords_ref, 3), rx=load(targets_ref, 0), ry=load(targets_ref, 1))
            out = []
            for name, total in zip(SUMS, sums):
                term = v[name] if len(name) == 2 else v[name[:2]] * v[name[2:]]
                out.append(total + (term[:8] + term[8:]))
            square = v["rx"] * v["rx"] + v["ry"] * v["ry"]
            out.append(sums[-1] + (square[:8] + square[8:]))
            return tuple(out)

        def chunks(k, sums):
            for i in range(CHUNKS):
                sums = chunk(k * CHUNKS + i, sums)
            return sums

        zero = jnp.zeros((8, NCOLS), F32)
        sums = (zero,) * len(SUMS) + (squares,)
        sums = lax.fori_loop(0, slots // (16 * CHUNKS), chunks, sums)
        squares = sums[-1]
        totals = {name: jnp.sum(s, axis=0, keepdims=True) for name, s in zip(SUMS, sums)}
        for row, name in enumerate(TABLE):
            if name == "0":
                line = jnp.zeros((1, NCOLS), F32)
            elif name in lines:
                line = lines[name][:, block * NCOLS : (block + 1) * NCOLS]
            elif name[0] == "-":
                line = -totals[name[1:]]
            else:
                line = totals[name]
            table[row : row + 1, lanes] = line
    return squares


def place_table(first_ref, chosen):
    pairs = first_ref.shape[1]
    first = jnp.broadcast_to(first_ref[...], (NCOLS, pairs))
    column = lax.broadcasted_iota(jnp.int32, (NCOLS, pairs), 0)
    for row in range(TILE_ROWS):
        start = ((row // ROWS_DEV + 2) * ROWS_WIDE + row % ROWS_DEV + 2) * NCOLS
        chosen[row] = jnp.where(first == column + start, 1.0, 0.0).astype(jnp.bfloat16)


def by_first_tile(chosen, table, store):
    values = table[...]
    high = values.astype(jnp.bfloat16)
    rest = values - high.astype(F32)
    middle = rest.astype(jnp.bfloat16)
    low = (rest - middle.astype(F32)).astype(jnp.bfloat16)
    parts = jnp.concatenate([high, middle, low], axis=0)
    height = values.shape[0]
    for row in range(TILE_ROWS):
        moved = lax.dot_general(
            parts, chosen[row], (((1,), (1,)), ((), ())), preferred_element_type=F32
        )
        moved = moved[:height] + moved[height : 2 * height] + moved[2 * height :]
        for group in range(len(GROUPS)):
            store(group, row, moved[8 * group : 8 * group + 8])


def row_key(block, row):
    section, band = block // 3 - 1, block % 3 - 1
    return (section * SEC_DEV + row // ROWS_DEV) * 256 + (band * ROWS_DEV + row % ROWS_DEV) * 16


def dynamic_key(block, row):
    section, band = block // 3 - 1, lax.rem(block, 3) - 1
    key = (section * SEC_DEV + row // ROWS_DEV) * 256 + (band * ROWS_DEV + row % ROWS_DEV) * 16
    return key.astype(F32)


def reach(block, row, target_block, target_row):
    section = (target_block // 3 - block // 3) * SEC_DEV + target_row // 2 - row // 2
    across = (target_block % 3 - block % 3) * ROWS_DEV + target_row % 2 - row % 2
    return abs(section) <= 2 and abs(across) <= 2


def turn(value, shift):
    return pltpu.roll(value, shift % NCOLS, 1) if shift else value


def own_keys(terms, moments, keys, moved):
    for row in range(TILE_ROWS):
        code = jnp.broadcast_to(moments[4, 0, row, 6:7, :], (8, NCOLS)) + float(row_key(4, row))
        for i, shift in enumerate(SHIFTS):
            keys[16 + row, i] = turn(code, shift) - float(shift)
            moved[row, i] = turn(terms[row], shift)


def scatter_to(block, keys, moved, out):
    for target in range(TILE_ROWS):
        total = jnp.zeros((8, NCOLS), F32)
        here = float(row_key(block, target))
        for row in range(TILE_ROWS):
            if reach(4, row, block, target):
                for i in range(5):
                    total = total + jnp.where(keys[16 + row, i] == here, moved[row, i], 0.0)
        out(target, total)


def gather_blocks(moments, keys):
    def step(block, totals):
        totals = list(totals)
        for row in range(TILE_ROWS):
            value = moments[block, 1, row]
            code = jnp.broadcast_to(moments[block, 0, row, 6:7, :], (8, NCOLS))
            code = code + dynamic_key(block, row)
            for i, shift in enumerate(SHIFTS):
                key = turn(code, shift) - float(shift)
                keys[block * TILE_ROWS + row, i] = key
                part = turn(value, shift)
                for t in range(TILE_ROWS):
                    hit = key == float(row_key(4, t))
                    totals[t] = totals[t] + jnp.where(hit, part, 0.0)
        return tuple(totals)

    return lax.fori_loop(0, 9, step, (jnp.zeros((8, NCOLS), F32),) * TILE_ROWS)


def own_blocks(block, g):
    upper, lower = halves(block)
    line = lax.rem(lax.broadcasted_iota(jnp.int32, (8, NCOLS), 0), 3)
    xx, xy, yy = (row_of(lower, k, k) for k in range(3))
    x, y = (row_of(upper, k, k) for k in range(2))
    first = jnp.where(line == 0, xx, jnp.where(line == 1, xy, jnp.where(line == 2, x, 0.0)))
    second = jnp.where(line == 0, xy, jnp.where(line == 1, yy, jnp.where(line == 2, y, 0.0)))
    return first * row_of(g, 0, 3) + second * row_of(g, 1, 4) + upper * row_of(g, 2, 5)


def apply_pairs(field, moments, local, keys, landed):
    def step(block, carry):
        far, totals = list(carry[:20]), list(carry[20:])
        for row in range(TILE_ROWS):
            g = field[block, row]
            known = isinstance(block, int)
            here = float(row_key(block, row)) if known else dynamic_key(block, row)
            near = [t for t in range(TILE_ROWS) if not known or reach(block, row, 4, t)]
            for t in near:
                for i in range(5):
                    far[t * 5 + i] = jnp.where(keys[16 + t, i] == here, g, far[t * 5 + i])
            by_a, by_b = halves(moments[block, 0, row])
            by_c, _ = halves(moments[block, 1, row])
            value = by_a * row_of(g, 0, 3) + by_b * row_of(g, 1, 4) + by_c * row_of(g, 2, 5)
            for i, shift in enumerate(SHIFTS):
                part = turn(value, shift)
                key = keys[block * TILE_ROWS + row, i]
                for t in near:
                    hit = key == float(row_key(4, t))
                    totals[t] = totals[t] + jnp.where(hit, part, 0.0)
        return tuple(far) + tuple(totals)

    def edge(k, carry):
        landed(2 * k + 1)
        return step(2 * k + 1, carry)

    carry = step(4, (jnp.zeros((8, NCOLS), F32),) * 24)
    carry = lax.fori_loop(0, len(EDGES), edge, carry)
    for block in CORNERS:
        landed(block)
        carry = step(block, carry)
    out = []
    for t in range(TILE_ROWS):
        far = carry[t * 5 + 2]
        for i, shift in enumerate(SHIFTS):
            if shift:
                far = far + turn(carry[t * 5 + i], -shift)
        by_a, by_b = halves(local[2, t])
        by_c, _ = halves(local[1, t])
        near = by_a * row_of(far, 0, 3) + by_b * row_of(far, 1, 4) + by_c * row_of(far, 2, 5)
        out.append(near + carry[20 + t])
    return out


def kernel(
    sections,
    bands,
    group_one,
    coords_ref,
    targets_ref,
    first,
    second,
    count,
    gradient_ref,
    product_ref,
    solution_scale_ref,
    product_scale_ref,
    gradient_scale_ref,
    coords,
    targets,
    chosen,
    table,
    terms,
    folded,
    arrived,
    moments,
    local,
    keys,
    moved,
    field,
    sums_one,
    sums_two,
    load_sems,
    terms_send,
    terms_recv,
    moments_send,
    moments_recv,
    field_send,
    field_recv,
    sums_send,
    sums_recv,
    met,
):
    sec = lax.axis_index("sec")
    band = lax.axis_index("band")
    place = lax.rem(sec, group_one)
    base = sec - place
    group = lax.div(sec, group_one)

    def neighbour(a, b):
        return (lax.rem(sec + a + sections, sections), lax.rem(band + b + bands, bands))

    loads = []

    def load(source, target):
        loads.append(pltpu.make_async_copy(source, target, load_sems.at[len(loads)]))
        loads[-1].start()

    blocks = coords_ref.shape[2] // NCOLS
    for i in range(blocks):
        lanes = pl.ds(i * NCOLS, NCOLS)
        load(coords_ref.at[:, :, lanes], coords.at[:, :, lanes])
        load(targets_ref.at[:, :, lanes], targets.at[:, :, lanes])
    groups = sections // group_one

    def far_first(k, count):
        return count // 2 + (2 * lax.rem(k, 2) - 1) * lax.div(k + 1, 2)

    def each_peer_one(act):
        def step(k, carry):
            act((base + lax.rem(place + far_first(k, group_one), group_one), band))
            return carry

        lax.fori_loop(0, group_one - 1, step, 0)

    def each_peer_two(act):
        def step(k, carry):
            other = lax.rem(group + far_first(k, groups), groups) * group_one + place
            for x in range(bands):
                act((other, x))
            return carry

        lax.fori_loop(0, groups - 1, step, 0)
        for x in range(1, bands):
            act((sec, lax.rem(band + x, bands)))

    def half(count):
        return (count // 2 + 1) // 2

    def each_relay(act):
        for d in range(1, half(group_one) + 1):
            for step in (d, group_one - d):
                act((base + lax.rem(place + step, group_one), band))
        for d in range(-half(groups), half(groups) + 1):
            other = lax.rem(group + d + groups, groups) * group_one + place
            for x in range(-half(bands), half(bands) + 1):
                if (d, x) != (0, 0):
                    act((other, lax.rem(band + x + bands, bands)))

    relays = 2 * half(group_one) + (2 * half(groups) + 1) * (2 * half(bands) + 1) - 1

    def signal(semaphore, device):
        pl.semaphore_signal(semaphore, inc=1, device_id=device, device_id_type=MESH)

    barrier = pltpu.get_barrier_semaphore()
    each_relay(functools.partial(signal, barrier))
    for a, b in NEIGHBOURS:
        signal(barrier, neighbour(a, b))

    place_table(first, chosen)

    def ready(i):
        loads[2 * i].wait()
        loads[2 * i + 1].wait()

    squares = pair_tables(coords, targets, first, second, count, table, ready)

    def store(group, tile_row, value):
        if group == 0:
            terms[tile_row] = value
        elif group < 3:
            moments[4, group - 1, tile_row] = value
        else:
            local[group - 3, tile_row] = value

    by_first_tile(chosen, table, store)
    own_keys(terms, moments, keys, moved)
    gradient = [None] * TILE_ROWS
    for block in range(9):

        def put(t, value, block=block):
            if block == 4:
                gradient[t] = value + local[0, t]
            else:
                folded[block, t] = value

        scatter_to(block, keys, moved, put)

    pl.semaphore_wait(barrier, 8 + relays)

    def send(source, target, send_sem, recv_sem, i, part=lambda ref: ref.at[:, 0:6]):
        a, b = NEIGHBOURS[i]
        copy = pltpu.make_async_remote_copy(
            src_ref=source,
            dst_ref=part(target.at[(1 - a) * 3 + 1 - b]),
            send_sem=send_sem.at[i],
            recv_sem=recv_sem.at[(1 - a) * 3 + 1 - b],
            device_id=neighbour(a, b),
            device_id_type=MESH,
        )
        copy.start()
        return copy

    def landed(ref, sem):
        pltpu.make_async_copy(ref, ref, sem).wait()

    terms_copies = []
    for i, (a, b) in enumerate(NEIGHBOURS):
        source = folded.at[(a + 1) * 3 + b + 1, :, 0:6]
        terms_copies.append(send(source, arrived, terms_send, terms_recv, i))
    moments_copies = []
    for i in range(8):
        moments_copies.append(send(moments.at[4], moments, moments_send, moments_recv, i, lambda ref: ref))

    each_relay(functools.partial(signal, met))

    for block in EDGES + CORNERS:
        landed(arrived.at[block, :, 0:6], terms_recv.at[block])
        for t in range(TILE_ROWS):
            gradient[t] = gradient[t] + arrived[block, t]
    held = lax.broadcasted_iota(jnp.int32, (8, NCOLS), 0) < 6
    for t in range(TILE_ROWS):
        gradient[t] = jnp.where(held, gradient[t], 0.0)
        field[4, t] = gradient[t]
    field_copies = []
    for i in range(8):
        field_copies.append(send(field.at[4, :, 0:6], field, field_send, field_recv, i))

    for block in EDGES + CORNERS:
        landed(moments.at[block], moments_recv.at[block])
    zero = jnp.zeros((8, NCOLS), F32)
    gg = zero
    own = []
    for t, block in enumerate(gather_blocks(moments, keys)):
        gg = gg + gradient[t] * gradient[t]
        own.append(own_blocks(block + local[1, t], gradient[t]))

    def whole(part):
        return jnp.sum(jnp.sum(part, axis=0, keepdims=True), axis=1, keepdims=True)

    lane = lax.broadcasted_iota(jnp.int32, (1, NCOLS), 1)
    line = jnp.where(lane == 0, whole(squares), jnp.where(lane == 1, whole(gg), 0.0))

    def field_landed(block):
        landed(field.at[block, :, 0:6], field_recv.at[block])

    others = apply_pairs(field, moments, local, keys, field_landed)
    wg, ww = zero, zero
    product = []
    for t in range(TILE_ROWS):
        w = jnp.where(held, own[t] - others[t], 0.0)
        product.append(w)
        wg = wg + w * gradient[t]
        ww = ww + w * w

    for k, part in ((2, wg), (3, ww)):
        line = jnp.where(lane == k, whole(part), line)

    def store_results():
        for t in range(TILE_ROWS):
            for k in range(6):
                gradient_ref[k, t : t + 1, :] = gradient[t][k : k + 1]
                product_ref[k, t : t + 1, :] = product[t][k : k + 1]

    def spread_sum(line, buffer, each_peer, mine, i, meanwhile):
        own = buffer.at[pl.ds(mine, 1), :]
        buffer[pl.ds(mine, 1), :] = line

        def send_to(device):
            pltpu.make_async_remote_copy(
                src_ref=own,
                dst_ref=own,
                send_sem=sums_send.at[i],
                recv_sem=sums_recv.at[i],
                device_id=device,
                device_id_type=MESH,
            ).start()

        each_peer(send_to)
        meanwhile()
        others = buffer.at[pl.ds(1, buffer.shape[0] - 1), :]
        pltpu.make_async_copy(others, others, sums_recv.at[i]).wait()
        return jnp.sum(buffer[...], axis=0, keepdims=True)

    pl.semaphore_wait(met, relays)
    line = spread_sum(line, sums_one, each_peer_one, place, 0, store_results)
    line = spread_sum(line, sums_two, each_peer_two, group * bands + band, 1, lambda: None)

    rr, gg, wg, ww = (jnp.broadcast_to(line[:, k : k + 1], (1, NCOLS)) for k in range(4))
    beta_one = jnp.sqrt(rr)
    norm_g = jnp.sqrt(gg)
    alpha_one = norm_g / beta_one
    beta_two_sq = wg / gg - alpha_one * alpha_one
    beta_two = jnp.sqrt(beta_two_sq)
    on_w = 1.0 / (norm_g * beta_two)
    on_g = -(alpha_one / (beta_one * beta_two) + beta_two / norm_g)
    scaled = on_g / on_w
    alpha_two = on_w * jnp.sqrt(ww + scaled * (2.0 * wg + scaled * gg))
    rho_sq = alpha_one * alpha_one + beta_two_sq
    first_scale = alpha_one * beta_one / (rho_sq * norm_g)
    root = math.sqrt(float(6 * TILE_ROWS * NCOLS * sections * bands))
    scale_w = root * on_w / alpha_two
    scale_g = root * (on_g / alpha_two - beta_two * alpha_two / (rho_sq * norm_g))
    solution_scale_ref[...] = first_scale
    product_scale_ref[...] = scale_w
    gradient_scale_ref[...] = scale_g

    for copies in (terms_copies, moments_copies, field_copies):
        for copy in copies:
            copy.wait_send()
    for i, buffer in enumerate((sums_one, sums_two)):
        others = buffer.at[pl.ds(1, buffer.shape[0] - 1), :]
        pltpu.make_async_copy(others, others, sums_send.at[i]).wait()


def solution(mesh):
    sections, bands = mesh.shape["sec"], mesh.shape["band"]
    group_one = 24 if sections % 24 == 0 else 2
    group_two = sections // group_one * bands

    def on_device(targets, coords, pair_first, pair_second, pair_count):
        slots, pairs = coords.shape[1], coords.shape[-1]
        vmem = pl.BlockSpec(memory_space=pltpu.VMEM)
        anywhere = pl.BlockSpec(memory_space=pl.ANY)
        shape = (6, TILE_ROWS, NCOLS)
        tile = (8, NCOLS)
        dma = pltpu.SemaphoreType.DMA
        gradient, product, *scales = pl.pallas_call(
            functools.partial(kernel, sections, bands, group_one),
            out_shape=tuple(jax.ShapeDtypeStruct(s, F32) for s in (shape, shape) + ((1, NCOLS),) * 3),
            in_specs=[anywhere] * 2 + [vmem] * 3,
            out_specs=(vmem,) * 5,
            scratch_shapes=[
                pltpu.VMEM((4, slots, pairs), coords.dtype),
                pltpu.VMEM((2, slots, pairs), targets.dtype),
                pltpu.VMEM((TILE_ROWS, NCOLS, pairs), jnp.bfloat16),
                pltpu.VMEM((8 * len(GROUPS), pairs), F32),
                pltpu.VMEM((TILE_ROWS,) + tile, F32),
                pltpu.VMEM((9, TILE_ROWS) + tile, F32),
                pltpu.VMEM((9, TILE_ROWS) + tile, F32),
                pltpu.VMEM((9, 2, TILE_ROWS) + tile, F32),
                pltpu.VMEM((3, TILE_ROWS) + tile, F32),
                pltpu.VMEM((9 * TILE_ROWS, 5) + tile, F32),
                pltpu.VMEM((TILE_ROWS, 5) + tile, F32),
                pltpu.VMEM((9, TILE_ROWS) + tile, F32),
                pltpu.VMEM((group_one, NCOLS), F32),
                pltpu.VMEM((group_two, NCOLS), F32),
            ]
            + [dma((2 * (pairs // NCOLS),))]
            + [dma((8,)), dma((9,))] * 3
            + [dma((2,))] * 2
            + [pltpu.SemaphoreType.REGULAR],
            compiler_params=pltpu.CompilerParams(
                collective_id=0, has_side_effects=True, vmem_limit_bytes=VMEM_BYTES
            ),
        )(
            coords.reshape(4, slots, pairs),
            targets.reshape(2, slots, pairs),
            pair_first.reshape(1, pairs),
            pair_second.reshape(1, pairs),
            pair_count.reshape(1, pairs),
        )
        first_scale, scale_w, scale_g = (scale[None] for scale in scales)
        results = (first_scale * gradient, scale_w * product + scale_g * gradient)
        return tuple(x.reshape(6, SEC_DEV, ROWS_DEV, NCOLS) for x in results)

    return jax.shard_map(
        on_device,
        mesh=mesh,
        in_specs=(
            P(None, None, "sec", "band", None),
            P(None, None, "sec", "band", None),
            P("sec", "band", None),
            P("sec", "band", None),
            P("sec", "band", None),
        ),
        out_specs=(P(None, "sec", "band", None), P(None, "sec", "band", None)),
        check_vma=False,
    )
```
